256 devices in a mesh: dp: 128 (over z, y, x), frame: 2 (over core).
Axes of the slice: x: 4, y: 4, z: 8, core: 2. Of those that a mesh axis runs over, the one named last changes fastest.
Arguments:
- queries: bfloat16 [131072, 1536], P(('dp', 'frame')), may hold values from -7 to 7
- keys: bfloat16 [131072, 1536], P(('dp', 'frame')), may hold values from -7 to 7
- values: bfloat16 [131072, 1536], P(('dp', 'frame')), may hold values from -6 to 6
- grad_out: bfloat16 [131072, 3072], P(('dp', 'frame')), may hold values from -6 to 6
- out_weight: bfloat16 [1536, 3072], P(('dp', 'frame')), may hold values from -0.109375 to 0.109375
- frame_clip: int32 [128, 8], P('dp'), may hold values from 0 to 3, as said below
- frame_rows: int32 [128, 8], P('dp'), may hold values from 3 to 8
- frame_cols: int32 [128, 8], P('dp'), may hold values from 6 to 16
Outputs:
- grad_queries: bfloat16 [131072, 1536], P(('dp', 'frame'))
- grad_keys: bfloat16 [131072, 1536], P(('dp', 'frame'))
- grad_values: bfloat16 [131072, 1536], P(('dp', 'frame'))
The draws below stay inside these ranges and needn't reach their ends.
Inputs may be any that keep to these rules, and one draw needn't show every extreme that they name: `frame_clip`: within a group clip numbers never fall. Half of the groups hold a long clip split by frames: frames a to 7 form one clip, with a at most 1, and the frames before a another. The other groups hold short clips, each whole on the frames of one device: the clip number changes between frames 4 - 1 and 4, and once inside each device's frames.
All inputs are finite; a program needn't handle non-finite values.
Results may differ from the reference program's by a relative error of at most 0.015.
Values may be sent and summed in bfloat16 or wider, within the bound.
No kernel may reach another device: no remote copies, remote signals or barrier semaphores. Data moves between devices by JAX's collectives and lax.ppermute only.
A program may use at most 192 MiB of HBM per device.

```python
import jax
import jax.numpy as jnp
from jax import lax

D = 3072
HEADS = 12
HEAD_DIM = 128
TILE_H = 8
TILE_W = 16
RADIUS = 3
FR = 4
HD = 1536
FRAMES = 8
NTOK = 131072
N_DP = 128


def draw_queries(key, part):
    key = jax.random.fold_in(key, 3)
    return jax.random.truncated_normal(key, -6.0, 6.0, (NTOK, HD), jnp.float32).astype(jnp.bfloat16)


def draw_keys(key, part):
    key = jax.random.fold_in(key, 4)
    return jax.random.truncated_normal(key, -6.0, 6.0, (NTOK, HD), jnp.float32).astype(jnp.bfloat16)


def draw_frame_clip(key, part):
    key = jax.random.fold_in(key, 9)
    kinds = jax.random.permutation(jax.random.fold_in(key, 1), N_DP) % 2
    starts = jax.random.randint(jax.random.fold_in(key, 2), (N_DP,), 0, FR - RADIUS + 1)
    first_cut = jax.random.randint(jax.random.fold_in(key, 3), (N_DP,), 1, FR)
    second_cut = jax.random.randint(jax.random.fold_in(key, 4), (N_DP,), 1, FR)
    frame_slots = jnp.arange(FRAMES, dtype=jnp.int32)[None, :]
    long_ids = (frame_slots >= starts[:, None]).astype(jnp.int32)
    short_ids = (frame_slots >= first_cut[:, None]).astype(jnp.int32) + (frame_slots >= FR).astype(jnp.int32) + (frame_slots >= FR + second_cut[:, None]).astype(jnp.int32)
    return jnp.where(kinds[:, None] == 1, long_ids, short_ids).astype(jnp.int32)


def touch_ends(values, key, least, top_value):
    longest = values.shape.index(max(values.shape))
    spots = []
    for shift in (0, 1):
        where = [jax.random.randint(jax.random.fold_in(key, axis), (), 0, length) for axis, length in enumerate(values.shape)]
        where[longest] = (where[longest] + shift) % values.shape[longest]
        spots.append(tuple(where))
    return values.at[spots[0]].set(least).at[spots[1]].set(top_value)


def levels(stream_key, dims, pieces, low, top_value):
    gain, own = 1.0, jax.random.fold_in(stream_key, 6)
    for axis_at, shards_of in pieces:
        steps = jnp.exp(jax.random.uniform(jax.random.fold_in(own, axis_at), (shards_of,), jnp.float32, low / len(pieces), top_value / len(pieces)))
        gain = gain * jnp.repeat(steps, dims[axis_at] // shards_of).reshape([-1 if axis == axis_at else 1 for axis in range(len(dims))])
    return gain


def gaussian(stream_key, dims, scale, bound, shards=(), kind=jnp.bfloat16):
    entries = scale * jax.random.normal(stream_key, dims, jnp.float32)
    if shards:
        entries = entries * levels(stream_key, dims, shards, -0.22, 0.18)
    return jnp.clip(entries, -bound, bound).astype(kind)


def setup_inputs(seed: int = 0) -> dict:
    key_list = jax.random.split(jax.random.key(seed), 9)
    return {
        "queries": draw_queries(jax.random.fold_in(key_list[8], 71), 0),
        "keys": draw_keys(jax.random.fold_in(key_list[8], 71), 0),
        "values": gaussian(key_list[2], (NTOK, HD), 1.0, 6.0, ((0, 256),)),
        "grad_out": gaussian(key_list[3], (NTOK, D), 1.0, 6.0, ((0, 256),)),
        "out_weight": gaussian(key_list[4], (HD, D), D ** -0.5, 0.109375, ((0, 256),)),
        "frame_clip": draw_frame_clip(jax.random.fold_in(key_list[8], 71), 0),
        "frame_rows": touch_ends(jax.random.randint(key_list[6], (N_DP, FRAMES), 3, TILE_H + 1), jax.random.fold_in(key_list[6], 1), 3, TILE_H).astype(jnp.int32),
        "frame_cols": touch_ends(jax.random.randint(key_list[7], (N_DP, FRAMES), 6, TILE_W + 1), jax.random.fold_in(key_list[7], 1), 6, TILE_W).astype(jnp.int32),
    }


def lookup(column_table, indices, frame_slots):
    hits = indices[..., None] == frame_slots
    return jnp.sum(jnp.where(hits, column_table, 0), axis=-1).astype(jnp.int32)


def window_masks(query_frames, clip_row, rows_row, cols_row):
    frame_total = clip_row.shape[0]
    frame_slots = jnp.arange(frame_total, dtype=jnp.int32)
    offsets = jnp.arange(2 * RADIUS + 1, dtype=jnp.int32) - RADIUS
    key_frames = query_frames[:, None] + offsets[None, :]
    inside = (key_frames >= 0) & (key_frames < frame_total)
    key_clip = lookup(clip_row, key_frames, frame_slots)
    query_clip = lookup(clip_row, query_frames, frame_slots)
    same_clip = inside & (key_clip == query_clip[:, None])
    cells = jnp.arange(TILE_H * TILE_W, dtype=jnp.int32)
    row_of = cells // TILE_W
    col_of = cells % TILE_W
    nearby = (jnp.abs(row_of[:, None] - row_of[None, :]) <= RADIUS) & (jnp.abs(col_of[:, None] - col_of[None, :]) <= RADIUS)
    key_rows = lookup(rows_row, key_frames, frame_slots)
    key_cols = lookup(cols_row, key_frames, frame_slots)
    key_valid = inside[:, :, None] & (row_of[None, None, :] < key_rows[:, :, None]) & (col_of[None, None, :] < key_cols[:, :, None])
    allowed = same_clip[:, None, :, None] & nearby[None, :, None, :] & key_valid[:, None, :, :]
    selfpair = (offsets == 0)[None, None, :, None] & (cells[:, None] == cells[None, :])[None, :, None, :]
    allowed = allowed | selfpair
    query_rows = lookup(rows_row, query_frames, frame_slots)
    query_cols = lookup(cols_row, query_frames, frame_slots)
    query_valid = (row_of[None, :] < query_rows[:, None]) & (col_of[None, :] < query_cols[:, None])
    return allowed, query_valid


def one_head(query_head, grad_head, pair_head, allowed):
    frame_count = query_head.shape[0]
    reach_len = 2 * RADIUS + 1
    key_window = jnp.stack([pair_head[0, offset:offset + frame_count] for offset in range(reach_len)], axis=1)
    value_window = jnp.stack([pair_head[1, offset:offset + frame_count] for offset in range(reach_len)], axis=1)
    scale = 1.0 / (HEAD_DIM ** 0.5)
    query_wide = query_head.astype(jnp.float32)
    grad_wide = grad_head.astype(jnp.float32)
    scores = jnp.einsum("fid,fojd->fioj", query_wide, key_window.astype(jnp.float32)) * scale
    scores = jnp.where(allowed, scores, -jnp.inf)
    row_top = jnp.max(scores, axis=(2, 3), keepdims=True)
    probs = jnp.exp(scores - row_top)
    probs = probs / jnp.sum(probs, axis=(2, 3), keepdims=True)
    probs_low = probs.astype(jnp.bfloat16)
    grad_probs = jnp.einsum("fid,fojd->fioj", grad_wide, value_window.astype(jnp.float32))
    delta = jnp.sum(probs * grad_probs, axis=(2, 3), keepdims=True)
    grad_scores = (scale * probs * (grad_probs - delta)).astype(jnp.bfloat16)
    grad_query = jnp.einsum("fioj,fojd->fid", grad_scores.astype(jnp.float32), key_window.astype(jnp.float32))
    key_terms = jnp.einsum("fioj,fid->fojd", grad_scores.astype(jnp.float32), query_wide)
    value_terms = jnp.einsum("fioj,fid->fojd", probs_low.astype(jnp.float32), grad_wide)
    key_grad = jnp.zeros((frame_count + 2 * RADIUS,) + key_terms.shape[2:], jnp.float32)
    value_grad = jnp.zeros((frame_count + 2 * RADIUS,) + key_terms.shape[2:], jnp.float32)
    for offset in range(reach_len):
        key_grad = key_grad.at[offset:offset + frame_count].add(key_terms[:, offset])
        value_grad = value_grad.at[offset:offset + frame_count].add(value_terms[:, offset])
    return grad_query, jnp.stack([key_grad, value_grad])


def reference(queries, keys, values, grad_out, out_weight, frame_clip, frame_rows, frame_cols):
    tile = TILE_H * TILE_W
    groups = frame_clip.shape[0]
    frame_total = frame_clip.shape[1]
    width = queries.shape[1]

    def one_group(group_inputs):
        query_group, key_group, value_group, grad_group, clip_row, rows_row, cols_row = group_inputs
        query_frames = jnp.arange(frame_total, dtype=jnp.int32)
        allowed, query_valid = window_masks(query_frames, clip_row, rows_row, cols_row)
        grad_attn = jnp.dot(grad_group, out_weight.T, preferred_element_type=jnp.float32).astype(jnp.bfloat16)
        grad_attn = grad_attn * query_valid.reshape(-1, 1).astype(jnp.bfloat16)
        query_heads = jnp.moveaxis(query_group.reshape(frame_total, tile, HEADS, HEAD_DIM), 2, 0)
        grad_heads = jnp.moveaxis(grad_attn.reshape(frame_total, tile, HEADS, HEAD_DIM), 2, 0)
        stacked = jnp.stack([key_group, value_group]).reshape(2, frame_total, tile, HEADS, HEAD_DIM)
        stacked = jnp.pad(stacked, ((0, 0), (RADIUS, RADIUS), (0, 0), (0, 0), (0, 0)))
        pair_heads = jnp.moveaxis(stacked, 3, 0)

        def head_step(head_inputs):
            return one_head(head_inputs[0], head_inputs[1], head_inputs[2], allowed)

        grad_query, pair_grad = lax.map(head_step, (query_heads, grad_heads, pair_heads))
        grad_query = jnp.moveaxis(grad_query, 0, 2).reshape(frame_total * tile, width)
        pair_grad = jnp.moveaxis(pair_grad, 0, 3)[:, RADIUS:RADIUS + frame_total].reshape(2, frame_total * tile, width)
        return grad_query.astype(jnp.bfloat16), pair_grad[0].astype(jnp.bfloat16), pair_grad[1].astype(jnp.bfloat16)

    shaped = (queries.reshape(groups, -1, width), keys.reshape(groups, -1, width), values.reshape(groups, -1, width),
              grad_out.reshape(groups, -1, grad_out.shape[1]), frame_clip, frame_rows, frame_cols)
    grad_queries, grad_keys, grad_values = lax.map(one_group, shaped)
    return grad_queries.reshape(-1, width), grad_keys.reshape(-1, width), grad_values.reshape(-1, width)
```

```python
import jax
import jax.numpy as jnp
from jax import lax
from jax.experimental import pallas as pl
from jax.experimental.pallas import tpu as pltpu
from jax.sharding import PartitionSpec as P

HEAD_DIM = 128
TILE_W = 16
TILE = 128
RADIUS = 3
FRAMES = 8
LOCAL = 512
GROUP = 1024
HALF = 768
WIDTH = 1536
DIM = 3072
PAIR = 2 * TILE
SCALE = 1.0 / HEAD_DIM**0.5
LOG2E = 1.4426950408889634

FIRST_KEY = (0, 0, 1, 3)
KEY_COUNT = (5, 7, 7, 5)
OFFSET = (0, 5, 12, 19)
SLOTS = 24
KEY_MOST = 7 * TILE
VMEM = 52 * 1024 * 1024

NT = (((1,), (1,)), ((), ()))
NN = (((1,), (0,)), ((), ()))


def dot(lhs, rhs, dims):
    return lax.dot_general(lhs, rhs, dims, preferred_element_type=jnp.float32)


def fill_bias(info, bias):
    key_cell = lax.broadcasted_iota(jnp.int32, (TILE, PAIR), 0)
    lane = lax.broadcasted_iota(jnp.int32, (TILE, PAIR), 1)
    query_cell = lane & (TILE - 1)
    key_row, key_col = key_cell >> 4, key_cell & (TILE_W - 1)
    near = (jnp.abs(key_row - (query_cell >> 4)) <= RADIUS) & (
        jnp.abs(key_col - (query_cell & (TILE_W - 1))) <= RADIUS
    )
    second = lane >= TILE
    for pair in range(4):
        left, right = 2 * pair, 2 * pair + 1
        for slot in range(KEY_COUNT[pair]):
            frame = FIRST_KEY[pair] + slot
            clip = info[1 + frame]
            left_same = (info[1 + left] == clip) & (abs(frame - left) <= RADIUS)
            right_same = (info[1 + right] == clip) & (abs(frame - right) <= RADIUS)
            linked = jnp.where(
                second, right_same.astype(jnp.int32), left_same.astype(jnp.int32)
            )
            allowed = (
                near
                & (linked > 0)
                & (key_row < info[9 + frame])
                & (key_col < info[17 + frame])
            )
            if frame == left:
                allowed = allowed | (key_cell == lane)
            if frame == right:
                allowed = allowed | (key_cell + TILE == lane)
            start = (OFFSET[pair] + slot) * TILE
            bias[start : start + TILE, :] = jnp.where(allowed, 0.0, -1e30)


def gather_rows(info, scratch, own, other):
    own_start = pl.multiple_of(info[0] * LOCAL, LOCAL)
    other_start = pl.multiple_of((1 - info[0]) * LOCAL, LOCAL)
    scratch[pl.ds(own_start, LOCAL), :] = own
    scratch[pl.ds(other_start, LOCAL), :] = other


def probs_kernel(info, q_own, q_other, k_own, k_other, probs, q_all, k_all, bias, logits):
    @pl.when(pl.program_id(0) == 0)
    def _():
        fill_bias(info, bias)

    gather_rows(info, q_all, q_own[...], q_other[...])
    gather_rows(info, k_all, k_own[...], k_other[...])
    for pair in range(4):
        query = q_all[pair * PAIR : (pair + 1) * PAIR, :]
        top = None
        for slot in range(KEY_COUNT[pair]):
            frame = FIRST_KEY[pair] + slot
            start = (OFFSET[pair] + slot) * TILE
            score = dot(k_all[frame * TILE : (frame + 1) * TILE, :], query, NT)
            score = score * (SCALE * LOG2E) + bias[start : start + TILE, :]
            logits[slot * TILE : (slot + 1) * TILE, :] = score
            part = jnp.max(score.reshape(TILE // 8, 8, PAIR), axis=0)
            top = part if top is None else jnp.maximum(top, part)
        top = jnp.max(top, axis=0, keepdims=True)
        total = None
        for slot in range(KEY_COUNT[pair]):
            rows = slice(slot * TILE, (slot + 1) * TILE)
            weight = jnp.exp2(logits[rows, :] - top)
            logits[rows, :] = weight
            part = jnp.sum(weight.reshape(TILE // 8, 8, PAIR), axis=0)
            total = part if total is None else total + part
        inverse = 1.0 / jnp.sum(total, axis=0, keepdims=True)
        for slot in range(KEY_COUNT[pair]):
            start = (OFFSET[pair] + slot) * TILE
            rows = slice(slot * TILE, (slot + 1) * TILE)
            probs[0, start : start + TILE, :] = (logits[rows, :] * inverse).astype(jnp.bfloat16)


def probs_call(info, q, q_other, k, k_other):
    own = pl.BlockSpec((LOCAL, HEAD_DIM), lambda head, info: (0, info[0] * 6 + head))
    return pl.pallas_call(
        probs_kernel,
        out_shape=jax.ShapeDtypeStruct((6, SLOTS * TILE, PAIR), jnp.bfloat16),
        grid_spec=pltpu.PrefetchScalarGridSpec(
            num_scalar_prefetch=1,
            grid=(6,),
            in_specs=[own] * 4,
            out_specs=pl.BlockSpec((1, SLOTS * TILE, PAIR), lambda head, info: (head, 0, 0)),
            scratch_shapes=[
                pltpu.VMEM((GROUP, HEAD_DIM), jnp.bfloat16),
                pltpu.VMEM((GROUP, HEAD_DIM), jnp.bfloat16),
                pltpu.VMEM((SLOTS * TILE, PAIR), jnp.float32),
                pltpu.VMEM((KEY_MOST, PAIR), jnp.float32),
            ],
        ),
        compiler_params=pltpu.CompilerParams(vmem_limit_bytes=VMEM),
        cost_estimate=pl.CostEstimate(
            flops=6 * 2 * SLOTS * TILE * PAIR * HEAD_DIM,
            bytes_accessed=12_000_000,
            transcendentals=6 * SLOTS * TILE * PAIR,
        ),
        name="probs",
    )(info, q, q_other, k, k_other)


def masked_grad(info, grad_all, start_frame, grad_out, weight):
    grad = dot(grad_out, weight, NT)
    cell = lax.broadcasted_iota(jnp.int32, (TILE, PAIR), 0)
    row, col = cell >> 4, cell & (TILE_W - 1)
    for step in range(4):
        frame = start_frame + step
        valid = (row < info[9 + frame]) & (col < info[17 + frame])
        part = grad[step * TILE : (step + 1) * TILE, :]
        part = jnp.where(valid, part, 0.0).astype(jnp.bfloat16)
        grad_all[pl.ds(pl.multiple_of(frame * TILE, TILE), TILE), :] = part


def grads_kernel(
    info, g_own, g_other, weight, probs, q_own, q_other, k_own, k_other, v_own, v_other,
    dq_own, dk_own, dv_own, dq_send, dk_send, dv_send,
    grad_all, q_all, k_all, v_all, grad_probs, grad_scores, dq_all, dk_all, dv_all,
):
    me = info[0]
    masked_grad(info, grad_all, me * 4, g_own[...], weight[...])
    masked_grad(info, grad_all, (1 - me) * 4, g_other[...], weight[...])
    gather_rows(info, q_all, q_own[...], q_other[...])
    gather_rows(info, k_all, k_own[...], k_other[...])
    gather_rows(info, v_all, v_own[...], v_other[...])
    for head in range(2):
        cols = slice(head * HEAD_DIM, (head + 1) * HEAD_DIM)
        key_turned = k_all[:, cols].T
        dk_all[...] = jnp.zeros_like(dk_all)
        dv_all[...] = jnp.zeros_like(dv_all)
        for pair in range(4):
            first, count = FIRST_KEY[pair], KEY_COUNT[pair]
            key_rows = slice(first * TILE, (first + count) * TILE)
            queries = slice(pair * PAIR, (pair + 1) * PAIR)
            grad = grad_all[queries, cols]
            delta = None
            for slot in range(count):
                frame = first + slot
                start = (OFFSET[pair] + slot) * TILE
                part = dot(v_all[frame * TILE : (frame + 1) * TILE, cols], grad, NT)
                grad_probs[slot * TILE : (slot + 1) * TILE, :] = part
                part = part * probs[head, start : start + TILE, :].astype(jnp.float32)
                part = jnp.sum(part.reshape(TILE // 8, 8, PAIR), axis=0)
                delta = part if delta is None else delta + part
            delta = jnp.sum(delta, axis=0, keepdims=True)
            for slot in range(count):
                rows = slice(slot * TILE, (slot + 1) * TILE)
                start = (OFFSET[pair] + slot) * TILE
                weights = probs[head, start : start + TILE, :].astype(jnp.float32)
                grad_scores[rows, :] = (weights * (grad_probs[rows, :] - delta)).astype(
                    jnp.bfloat16
                )
            scores = grad_scores[: count * TILE, :]
            start = OFFSET[pair] * TILE
            dq_turned = dot(key_turned[:, key_rows], scores, NN) * SCALE
            dq_all[queries, :] = dq_turned.T
            dk_all[key_rows, :] += dot(scores, q_all[queries, cols], NN)
            dv_all[key_rows, :] += dot(
                probs[head, start : start + count * TILE, :], grad, NN
            )
        own = pl.ds(pl.multiple_of(me * LOCAL, LOCAL), LOCAL)
        other = pl.ds(pl.multiple_of((1 - me) * LOCAL, LOCAL), LOCAL)
        dq_own[:, cols] = dq_all[own, :].astype(jnp.bfloat16)
        dk_own[:, cols] = (dk_all[own, :] * SCALE).astype(jnp.bfloat16)
        dv_own[:, cols] = dv_all[own, :].astype(jnp.bfloat16)
        dq_send[:, cols] = dq_all[other, :].astype(jnp.bfloat16)
        dk_send[:, cols] = (dk_all[other, :] * SCALE).astype(jnp.bfloat16)
        dv_send[:, cols] = dv_all[other, :].astype(jnp.bfloat16)


def grads_call(info, grad_out, grad_other, weight, probs, q, q_other, k, k_other, v, v_other):
    whole = pl.BlockSpec((LOCAL, DIM), lambda step, info: (0, 0))
    own = pl.BlockSpec((LOCAL, PAIR), lambda step, info: (0, info[0] * 3 + step))
    sent = pl.BlockSpec((LOCAL, PAIR), lambda step, info: (0, step))
    full = jax.ShapeDtypeStruct((LOCAL, WIDTH), jnp.bfloat16)
    half = jax.ShapeDtypeStruct((LOCAL, HALF), jnp.bfloat16)
    return pl.pallas_call(
        grads_kernel,
        out_shape=[full] * 3 + [half] * 3,
        grid_spec=pltpu.PrefetchScalarGridSpec(
            num_scalar_prefetch=1,
            grid=(3,),
            in_specs=[
                whole,
                whole,
                pl.BlockSpec((PAIR, DIM), lambda step, info: (info[0] * 3 + step, 0)),
                pl.BlockSpec((2, SLOTS * TILE, PAIR), lambda step, info: (step, 0, 0)),
            ]
            + [own] * 6,
            out_specs=[own] * 3 + [sent] * 3,
            scratch_shapes=[
                pltpu.VMEM((GROUP, PAIR), jnp.bfloat16),
                pltpu.VMEM((GROUP, PAIR), jnp.bfloat16),
                pltpu.VMEM((GROUP, PAIR), jnp.bfloat16),
                pltpu.VMEM((GROUP, PAIR), jnp.bfloat16),
                pltpu.VMEM((KEY_MOST, PAIR), jnp.float32),
                pltpu.VMEM((KEY_MOST, PAIR), jnp.bfloat16),
                pltpu.VMEM((GROUP, HEAD_DIM), jnp.float32),
                pltpu.VMEM((GROUP, HEAD_DIM), jnp.float32),
                pltpu.VMEM((GROUP, HEAD_DIM), jnp.float32),
            ],
        ),
        compiler_params=pltpu.CompilerParams(vmem_limit_bytes=VMEM),
        cost_estimate=pl.CostEstimate(
            flops=6 * 8 * SLOTS * TILE * PAIR * HEAD_DIM + 2 * GROUP * HALF * DIM,
            bytes_accessed=30_000_000,
            transcendentals=0,
        ),
        name="grads",
    )(info, grad_out, grad_other, weight, probs, q, q_other, k, k_other, v, v_other)


def merge_kernel(info, *refs):
    arrived, outs, sems = refs[3:6], refs[6:9], refs[9]
    start = pl.multiple_of((1 - info[0]) * HALF, HALF)
    copies = [
        pltpu.make_async_copy(src, dst.at[:, pl.ds(start, HALF)], sems.at[i])
        for i, (src, dst) in enumerate(zip(arrived, outs))
    ]
    for copy in copies:
        copy.start()
    for copy in copies:
        copy.wait()


def merge_call(info, own, arrived):
    full = jax.ShapeDtypeStruct((LOCAL, WIDTH), jnp.bfloat16)
    return pl.pallas_call(
        merge_kernel,
        out_shape=[full] * 3,
        grid_spec=pltpu.PrefetchScalarGridSpec(
            num_scalar_prefetch=1,
            grid=(1,),
            in_specs=[pl.BlockSpec(memory_space=pl.ANY)] * 6,
            out_specs=[pl.BlockSpec(memory_space=pl.ANY)] * 3,
            scratch_shapes=[pltpu.SemaphoreType.DMA((3,))],
        ),
        input_output_aliases={1: 0, 2: 1, 3: 2},
        name="merge",
    )(info, *own, *arrived)


def swap(value):
    return lax.ppermute(value, "frame", [(0, 1), (1, 0)])


def on_device(queries, keys, values, grad_out, out_weight, frame_clip, frame_rows, frame_cols):
    me = lax.axis_index("frame").astype(jnp.int32)
    info = jnp.concatenate([me.reshape(1), frame_clip[0], frame_rows[0], frame_cols[0]])
    weight = lax.all_gather(out_weight, ("dp", "frame"), axis=0, tiled=True)
    q_other, k_other, v_other, g_other = (swap(x) for x in (queries, keys, values, grad_out))
    probs = probs_call(info, queries, q_other, keys, k_other)
    outs = grads_call(
        info, grad_out, g_other, weight, probs, queries, q_other, keys, k_other, values, v_other
    )
    return tuple(merge_call(info, outs[:3], [swap(x) for x in outs[3:]]))


def solution(mesh):
    split = P(("dp", "frame"), None)
    table = P("dp", None)
    return jax.shard_map(
        on_device,
        mesh=mesh,
        in_specs=(split,) * 5 + (table,) * 3,
        out_specs=(split,) * 3,
        check_vma=False,
    )
```

```python
import functools

import jax
import jax.numpy as jnp
import numpy as np
from jax import lax
from jax.experimental import pallas as pl
from jax.experimental.pallas import tpu as pltpu
from jax.sharding import PartitionSpec as P

HEAD_DIM = 128
TILE_W = 16
TILE = 128
RADIUS = 3
FRAMES = 8
LOCAL = 512
GROUP = 1024
HALF = 768
WIDTH = 1536
DIM = 3072
PAIR = 2 * TILE
SCALE = 1.0 / HEAD_DIM**0.5
LOG2E = 1.4426950408889634

FIRST_KEY = (0, 0, 1, 3)
KEY_COUNT = (5, 7, 7, 5)
OFFSET = (0, 5, 12, 19)
SLOTS = 24
KEY_MOST = 7 * TILE
VMEM = 24 * 1024 * 1024

CHUNK = 48
SLAB = 192
NZ, NY, NX = 8, 4, 4
SLOT_SHIFT = (0, 1, 3, 2)
ME, MINE, THEIRS, INNER, ROWS_EARLY, ROWS_LATE = range(6)

NT = (((1,), (1,)), ((), ()))
NN = (((1,), (0,)), ((), ()))


def dot(lhs, rhs, dims):
    return lax.dot_general(lhs, rhs, dims, preferred_element_type=jnp.float32)


def fill_bias(clips, valid_rows, valid_cols, bias):
    key_cell = lax.broadcasted_iota(jnp.int32, (TILE, PAIR), 0)
    lane = lax.broadcasted_iota(jnp.int32, (TILE, PAIR), 1)
    query_cell = lane & (TILE - 1)
    key_row, key_col = key_cell >> 4, key_cell & (TILE_W - 1)
    near = (jnp.abs(key_row - (query_cell >> 4)) <= RADIUS) & (
        jnp.abs(key_col - (query_cell & (TILE_W - 1))) <= RADIUS
    )
    second = lane >= TILE
    for pair in range(4):
        left, right = 2 * pair, 2 * pair + 1
        for slot in range(KEY_COUNT[pair]):
            frame = FIRST_KEY[pair] + slot
            clip = clips[0, frame]
            left_same = (clips[0, left] == clip) & (abs(frame - left) <= RADIUS)
            right_same = (clips[0, right] == clip) & (abs(frame - right) <= RADIUS)
            linked = jnp.where(
                second, right_same.astype(jnp.int32), left_same.astype(jnp.int32)
            )
            allowed = (
                near
                & (linked > 0)
                & (key_row < valid_rows[0, frame])
                & (key_col < valid_cols[0, frame])
            )
            if frame == left:
                allowed = allowed | (key_cell == lane)
            if frame == right:
                allowed = allowed | (key_cell + TILE == lane)
            start = (OFFSET[pair] + slot) * TILE
            bias[start : start + TILE, :] = jnp.where(allowed, 0.0, -1e30)


def gather_rows(info, scratch, own, other):
    own_start = pl.multiple_of(info[ME] * LOCAL, LOCAL)
    other_start = pl.multiple_of((1 - info[ME]) * LOCAL, LOCAL)
    scratch[pl.ds(own_start, LOCAL), :] = own
    scratch[pl.ds(other_start, LOCAL), :] = other


def probs_kernel(
    info, clips, valid_rows, valid_cols, q_own, k_own, q_other, k_other, slab,
    probs, slab_out, q_all, k_all, bias, logits,
):
    @pl.when(pl.program_id(0) == 0)
    def _():
        fill_bias(clips, valid_rows, valid_cols, bias)

    gather_rows(info, q_all, q_own[...], q_other[0])
    gather_rows(info, k_all, k_own[...], k_other[0])
    for pair in range(4):
        query = q_all[pair * PAIR : (pair + 1) * PAIR, :]
        top = None
        for slot in range(KEY_COUNT[pair]):
            frame = FIRST_KEY[pair] + slot
            start = (OFFSET[pair] + slot) * TILE
            score = dot(k_all[frame * TILE : (frame + 1) * TILE, :], query, NT)
            score = score * (SCALE * LOG2E) + bias[start : start + TILE, :]
            logits[slot * TILE : (slot + 1) * TILE, :] = score
            part = jnp.max(score.reshape(TILE // 8, 8, PAIR), axis=0)
            top = part if top is None else jnp.maximum(top, part)
        top = jnp.max(top, axis=0, keepdims=True)
        total = None
        for slot in range(KEY_COUNT[pair]):
            rows = slice(slot * TILE, (slot + 1) * TILE)
            weight = jnp.exp2(logits[rows, :] - top)
            logits[rows, :] = weight
            part = jnp.sum(weight.reshape(TILE // 8, 8, PAIR), axis=0)
            total = part if total is None else total + part
        inverse = 1.0 / jnp.sum(total, axis=0, keepdims=True)
        for slot in range(KEY_COUNT[pair]):
            start = (OFFSET[pair] + slot) * TILE
            rows = slice(slot * TILE, (slot + 1) * TILE)
            probs[0, start : start + TILE, :] = (logits[rows, :] * inverse).astype(jnp.bfloat16)


def probs_call(tables, q, k, others, slab):
    own = pl.BlockSpec((LOCAL, HEAD_DIM), lambda head, info, *_: (0, info[ME] * 6 + head))
    q_other, k_other = (
        pl.BlockSpec(
            (1, LOCAL, HEAD_DIM),
            functools.partial(lambda which, head, *_: (which, 0, head), which),
        )
        for which in range(2)
    )
    return pl.pallas_call(
        probs_kernel,
        out_shape=[
            jax.ShapeDtypeStruct((6, SLOTS * TILE, PAIR), jnp.bfloat16),
            jax.ShapeDtypeStruct(slab.shape, slab.dtype),
        ],
        grid_spec=pltpu.PrefetchScalarGridSpec(
            num_scalar_prefetch=4,
            grid=(6,),
            in_specs=[own, own, q_other, k_other, pl.BlockSpec(memory_space=pl.ANY)],
            out_specs=[
                pl.BlockSpec((1, SLOTS * TILE, PAIR), lambda head, *_: (head, 0, 0)),
                pl.BlockSpec(memory_space=pl.ANY),
            ],
            scratch_shapes=[
                pltpu.VMEM((GROUP, HEAD_DIM), jnp.bfloat16),
                pltpu.VMEM((GROUP, HEAD_DIM), jnp.bfloat16),
                pltpu.VMEM((SLOTS * TILE, PAIR), jnp.float32),
                pltpu.VMEM((KEY_MOST, PAIR), jnp.float32),
            ],
        ),
        compiler_params=pltpu.CompilerParams(vmem_limit_bytes=VMEM),
        cost_estimate=pl.CostEstimate(
            flops=6 * 2 * SLOTS * TILE * PAIR * HEAD_DIM,
            bytes_accessed=12_000_000,
            transcendentals=6 * SLOTS * TILE * PAIR,
        ),
        input_output_aliases={8: 1},
        name="probs",
    )(*tables, q, k, others, others, slab)


def project(info, valid_rows, valid_cols, grad_all, grad_own, grad_other, weight):
    cell = lax.broadcasted_iota(jnp.int32, (TILE, HEAD_DIM), 0)
    row, col = cell >> 4, cell & (TILE_W - 1)
    for begin, grad_out in ((info[ME] * 4, grad_own), ((1 - info[ME]) * 4, grad_other)):
        grad = dot(grad_out[...], weight, NT)
        for step in range(4):
            frame = begin + step
            valid = (row < valid_rows[0, frame]) & (col < valid_cols[0, frame])
            rows = pl.ds(pl.multiple_of(frame * TILE, TILE), TILE)
            for head in range(2):
                part = grad[step * TILE : (step + 1) * TILE, head * TILE : (head + 1) * TILE]
                grad_all[head, rows, :] = jnp.where(valid, part, 0.0).astype(jnp.bfloat16)


def place_weight(info, pieces, refs, weight):
    for (slab, slots), ref in zip(pieces, refs):
        for index, slot in enumerate(slots):
            chunk = lax.rem(info[INNER] + SLOT_SHIFT[slot], 4)
            start = pl.multiple_of(slab * SLAB + chunk * CHUNK, 16)
            weight[pl.ds(start, CHUNK), :] = ref[index]


def grads_kernel(
    pieces, row_slot, aliased, info, clips, valid_rows, valid_cols, *refs
):
    weight_refs, refs = refs[: len(pieces)], refs[len(pieces) + aliased :]
    grad_own, grad_other, probs = refs[:3]
    q_own, k_own, v_own, q_other, k_other, v_other = refs[3:9]
    dq_own, dk_own, dv_own, dq_send, dk_send, dv_send = refs[9:15]
    weight, grad_all, q_all, k_all, v_all, grad_probs, grad_scores = refs[15:22]
    dq_all, dk_all, dv_all = refs[22:]
    me = info[ME]
    step = pl.program_id(0)

    @pl.when(step == 0)
    def _():
        place_weight(info, pieces, weight_refs, weight)

    @pl.when(lax.rem(step, 2) == 0)
    def _():
        start = pl.multiple_of(info[row_slot] + step * HEAD_DIM, 64)
        rows = weight[pl.ds(start, PAIR), :]
        project(info, valid_rows, valid_cols, grad_all, grad_own, grad_other, rows)

    probs = probs.at[0]
    gather_rows(info, q_all, q_own[...], q_other[0])
    gather_rows(info, k_all, k_own[...], k_other[0])
    gather_rows(info, v_all, v_own[...], v_other[0])
    grads = grad_all.at[lax.rem(step, 2)]
    key_turned = k_all[...].T
    dk_all[...] = jnp.zeros_like(dk_all)
    dv_all[...] = jnp.zeros_like(dv_all)
    for pair in range(4):
        first, count = FIRST_KEY[pair], KEY_COUNT[pair]
        key_rows = slice(first * TILE, (first + count) * TILE)
        queries = slice(pair * PAIR, (pair + 1) * PAIR)
        grad = grads[queries, :]
        delta = None
        grad_probs[: count * TILE, :] = dot(v_all[key_rows, :], grad, NT)
        for slot in range(count):
            start = (OFFSET[pair] + slot) * TILE
            part = grad_probs[slot * TILE : (slot + 1) * TILE, :]
            part = part * probs[start : start + TILE, :].astype(jnp.float32)
            part = jnp.sum(part.reshape(TILE // 8, 8, PAIR), axis=0)
            delta = part if delta is None else delta + part
        delta = jnp.sum(delta, axis=0, keepdims=True)
        for slot in range(count):
            rows = slice(slot * TILE, (slot + 1) * TILE)
            start = (OFFSET[pair] + slot) * TILE
            weights = probs[start : start + TILE, :].astype(jnp.float32)
            grad_scores[rows, :] = (weights * (grad_probs[rows, :] - delta)).astype(jnp.bfloat16)
        scores = grad_scores[: count * TILE, :]
        start = OFFSET[pair] * TILE
        dq_turned = dot(key_turned[:, key_rows], scores, NN) * SCALE
        dq_all[queries, :] = dq_turned.T
        dk_all[key_rows, :] += dot(scores, q_all[queries, :], NN)
        dv_all[key_rows, :] += dot(probs[start : start + count * TILE, :], grad, NN)
    own = pl.ds(pl.multiple_of(me * LOCAL, LOCAL), LOCAL)
    other = pl.ds(pl.multiple_of((1 - me) * LOCAL, LOCAL), LOCAL)
    dq_own[...] = dq_all[own, :].astype(jnp.bfloat16)
    dk_own[...] = (dk_all[own, :] * SCALE).astype(jnp.bfloat16)
    dv_own[...] = dv_all[own, :].astype(jnp.bfloat16)
    dq_send[...] = dq_all[other, :].astype(jnp.bfloat16)
    dk_send[...] = (dk_all[other, :] * SCALE).astype(jnp.bfloat16)
    dv_send[...] = dv_all[other, :].astype(jnp.bfloat16)


def grads_call(tables, pieces, earlier, begin, heads, row_slot, tokens, probs):
    def head_at(step, info):
        return lax.rem(info[MINE] + begin + step, 6)

    whole = pl.BlockSpec(memory_space=pltpu.VMEM)
    own = pl.BlockSpec(
        (LOCAL, HEAD_DIM), lambda step, info, *_: (0, info[ME] * 6 + head_at(step, info))
    )
    other = [
        pl.BlockSpec(
            (1, LOCAL, HEAD_DIM),
            functools.partial(
                lambda which, step, info, *_: (which, 0, head_at(step, info)), which
            ),
        )
        for which in range(3)
    ]
    sent = pl.BlockSpec((LOCAL, HEAD_DIM), lambda step, *_: (0, step))
    anywhere = pl.BlockSpec(memory_space=pl.ANY)
    full = jax.ShapeDtypeStruct((LOCAL, WIDTH), jnp.bfloat16)
    send = jax.ShapeDtypeStruct((LOCAL, heads * HEAD_DIM), jnp.bfloat16)
    arrays = [piece for _, _, piece in pieces]
    layout = tuple((slab, slots) for slab, slots, _ in pieces)
    return pl.pallas_call(
        lambda *refs: grads_kernel(layout, row_slot, len(earlier), *refs),
        out_shape=[full] * 3 + [send] * 3,
        grid_spec=pltpu.PrefetchScalarGridSpec(
            num_scalar_prefetch=4,
            grid=(heads,),
            in_specs=[whole] * len(arrays)
            + [anywhere] * len(earlier)
            + [whole] * 2
            + [
                pl.BlockSpec(
                    (1, SLOTS * TILE, PAIR), lambda step, info, *_: (head_at(step, info), 0, 0)
                )
            ]
            + [own] * 3
            + other,
            out_specs=[own] * 3 + [sent] * 3,
            scratch_shapes=[
                pltpu.VMEM((3 * SLAB, DIM), jnp.bfloat16),
                pltpu.VMEM((2, GROUP, HEAD_DIM), jnp.bfloat16),
                pltpu.VMEM((GROUP, HEAD_DIM), jnp.bfloat16),
                pltpu.VMEM((GROUP, HEAD_DIM), jnp.bfloat16),
                pltpu.VMEM((GROUP, HEAD_DIM), jnp.bfloat16),
                pltpu.VMEM((KEY_MOST, PAIR), jnp.float32),
                pltpu.VMEM((KEY_MOST, PAIR), jnp.bfloat16),
                pltpu.VMEM((GROUP, HEAD_DIM), jnp.float32),
                pltpu.VMEM((GROUP, HEAD_DIM), jnp.float32),
                pltpu.VMEM((GROUP, HEAD_DIM), jnp.float32),
            ],
        ),
        input_output_aliases={4 + len(arrays) + i: i for i in range(len(earlier))},
        compiler_params=pltpu.CompilerParams(vmem_limit_bytes=VMEM),
        cost_estimate=pl.CostEstimate(
            flops=heads * (8 * SLOTS * TILE * PAIR * HEAD_DIM + 2 * GROUP * HEAD_DIM * DIM),
            bytes_accessed=5_000_000 * heads,
            transcendentals=0,
        ),
        name="grads",
    )(*tables, *arrays, *earlier, *tokens[:2], probs, *tokens[2:5], *[tokens[5]] * 3)


def merge_kernel(info, *refs):
    arrived, outs, sems = refs[3:9], refs[9:12], refs[12]
    copies = []
    for begin, heads, parts in ((0, 4, arrived[:3]), (4, 2, arrived[3:])):
        for step in range(heads):
            head = (1 - info[ME]) * 6 + lax.rem(info[THEIRS] + begin + step, 6)
            cols = pl.ds(pl.multiple_of(head * HEAD_DIM, HEAD_DIM), HEAD_DIM)
            for part, out in zip(parts, outs):
                copies.append(
                    pltpu.make_async_copy(
                        part.at[:, step * HEAD_DIM : (step + 1) * HEAD_DIM],
                        out.at[:, cols],
                        sems.at[len(copies)],
                    )
                )
    for copy in copies:
        copy.start()
    for copy in copies:
        copy.wait()


def merge_call(info, own, arrived):
    full = jax.ShapeDtypeStruct((LOCAL, WIDTH), jnp.bfloat16)
    return pl.pallas_call(
        merge_kernel,
        out_shape=[full] * 3,
        grid_spec=pltpu.PrefetchScalarGridSpec(
            num_scalar_prefetch=1,
            grid=(1,),
            in_specs=[pl.BlockSpec(memory_space=pl.ANY)] * 3
            + [pl.BlockSpec(memory_space=pltpu.VMEM)] * 6,
            out_specs=[pl.BlockSpec(memory_space=pl.ANY)] * 3,
            scratch_shapes=[pltpu.SemaphoreType.DMA((18,))],
        ),
        input_output_aliases={1: 0, 2: 1, 3: 2},
        compiler_params=pltpu.CompilerParams(vmem_limit_bytes=VMEM),
        name="merge",
    )(info, *own, *arrived)


def place_table():
    table = np.zeros((NZ * NY * NX, 2, 6), np.int32)
    for dp in range(NZ * NY * NX):
        y, quarter = dp // NX % NY, dp // (NY * NX) % 4
        for core in range(2):
            outer, inner = (y, quarter) if core == 0 else (quarter, y)
            begin = (5, 0, 2, 3)
            rows = 64 * (1 - outer % 2)
            table[dp, core] = (core, begin[outer], begin[inner], inner, rows, 128 + rows)
    return table.reshape(-1, 6)


def place(z, y, x, core):
    return (((z % NZ) * NY + y % NY) * NX + x % NX) * 2 + core


def move(value, source):
    places = [
        (z, y, x, core) for z in range(NZ) for y in range(NY) for x in range(NX) for core in range(2)
    ]
    pairs = [(source(*taker), place(*taker)) for taker in places]
    return lax.ppermute(value, ("dp", "frame"), pairs)


def first_rows(step):
    def source(z, y, x, core):
        inner, outer = (z % 4, y) if core == 0 else (y, z % 4)
        return 128 * core + 8 * (4 * outer + inner) + 2 * x + ((z // 4) ^ step)

    return source


def along(last, distance):
    def source(z, y, x, core):
        if (core == 0) == last:
            return place(z, y + distance, x, core)
        return place(z + distance, y, x, core)

    return source


def line_rows(out_weight, z):
    x_lines = [
        [(z * NY + y) * NX + x for x in range(NX)] for z in range(NZ) for y in range(NY)
    ]
    even, odd = (move(out_weight, first_rows(step)) for step in range(2))
    rows = jnp.stack([jnp.where(z >= 4, odd, even), jnp.where(z >= 4, even, odd)])
    return lax.all_to_all(
        jnp.broadcast_to(rows[None], (NX,) + rows.shape),
        "dp",
        0,
        0,
        axis_index_groups=x_lines,
        tiled=True,
    ).reshape(1, CHUNK, DIM)


def beside_rows(rows):
    return [move(rows, along(False, distance)) for distance in (1, -1, 2)]


def far_slab(after_low, before_high):
    return move(after_low, along(True, 1)), move(before_high, along(True, -1))


def swap(value):
    return lax.ppermute(value, "frame", [(0, 1), (1, 0)])


def other_half(value, me):
    return jnp.where(me == 0, value[:, HALF:], value[:, :HALF])


def on_device(queries, keys, values, grad_out, out_weight, frame_clip, frame_rows, frame_cols):
    me = lax.axis_index("frame")
    dp = lax.axis_index("dp")
    info = lax.dynamic_index_in_dim(jnp.asarray(place_table()), dp * 2 + me, 0, keepdims=False)
    tables = (info, frame_clip, frame_rows, frame_cols)
    g_other = swap(grad_out)
    others = swap(jnp.stack([other_half(x, me) for x in (queries, keys, values)]))
    rows = line_rows(out_weight, dp // (NY * NX))
    slab = jnp.concatenate([rows] + beside_rows(rows))
    after_low, before_high = move(slab[:2], along(True, 1)), move(slab[2:], along(True, -1))
    probs, slab = probs_call(tables, queries, keys, others, slab)
    after_high, before_low = move(slab[2:], along(True, 1)), move(slab[:2], along(True, -1))
    far_low, far_high = far_slab(after_low, before_high)
    tokens = (grad_out, g_other, queries, keys, values, others)
    low, high, both = (0, 1), (2, 3), (0, 1, 2, 3)
    pieces = (
        (0, low, before_low),
        (0, high, before_high),
        (1, both, slab),
        (2, low, after_low),
        (2, high, after_high),
    )
    early = grads_call(tables, pieces, (), 0, 4, ROWS_EARLY, tokens, probs)
    pieces = (
        (0, low, after_low),
        (0, high, after_high),
        (1, low, far_low),
        (1, high, far_high),
        (2, low, before_low),
        (2, high, before_high),
    )
    late = grads_call(tables, pieces, tuple(early[:3]), 4, 2, ROWS_LATE, tokens, probs)
    sent = [swap(x) for x in early[3:]] + [swap(x) for x in late[3:]]
    return tuple(merge_call(info, late[:3], sent))


def solution(mesh):
    split = P(("dp", "frame"), None)
    table = P("dp", None)
    return jax.shard_map(
        on_device,
        mesh=mesh,
        in_specs=(split,) * 5 + (table,) * 3,
        out_specs=(split,) * 3,
        check_vma=False,
    )
```

```python
import functools

import jax
import jax.numpy as jnp
import numpy as np
from jax import lax
from jax.experimental import pallas as pl
from jax.experimental.pallas import tpu as pltpu
from jax.sharding import PartitionSpec as P

HEAD_DIM = 128
TILE_W = 16
TILE = 128
RADIUS = 3
FRAMES = 8
LOCAL = 512
GROUP = 1024
HALF = 768
WIDTH = 1536
DIM = 3072
PAIR = 2 * TILE
SCALE = 1.0 / HEAD_DIM**0.5
LOG2E = 1.4426950408889634

FIRST_KEY = (0, 0, 1, 3)
KEY_COUNT = (5, 7, 7, 5)
OFFSET = (0, 5, 12, 19)
SLOTS = 24
KEY_MOST = 7 * TILE
VMEM = 26 * 1024 * 1024

CHUNK = 48
SLAB = 192
NZ, NY, NX = 8, 4, 4
SLOT_SHIFT = (0, 1, 3, 2)
ME, MINE, THEIRS, INNER, ROWS_EARLY, ROWS_LATE = range(6)

NT = (((1,), (1,)), ((), ()))
TN = (((0,), (0,)), ((), ()))
NN = (((1,), (0,)), ((), ()))


def dot(lhs, rhs, dims):
    return lax.dot_general(lhs, rhs, dims, preferred_element_type=jnp.float32)


def fill_bias(clips, valid_rows, valid_cols, bias):
    key_cell = lax.broadcasted_iota(jnp.int32, (TILE, PAIR), 0)
    lane = lax.broadcasted_iota(jnp.int32, (TILE, PAIR), 1)
    query_cell = lane & (TILE - 1)
    key_row, key_col = key_cell >> 4, key_cell & (TILE_W - 1)
    near = (jnp.abs(key_row - (query_cell >> 4)) <= RADIUS) & (
        jnp.abs(key_col - (query_cell & (TILE_W - 1))) <= RADIUS
    )
    second = lane >= TILE
    for pair in range(4):
        left, right = 2 * pair, 2 * pair + 1
        for slot in range(KEY_COUNT[pair]):
            frame = FIRST_KEY[pair] + slot
            clip = clips[0, frame]
            left_same = (clips[0, left] == clip) & (abs(frame - left) <= RADIUS)
            right_same = (clips[0, right] == clip) & (abs(frame - right) <= RADIUS)
            linked = jnp.where(
                second, right_same.astype(jnp.int32), left_same.astype(jnp.int32)
            )
            allowed = (
                near
                & (linked > 0)
                & (key_row < valid_rows[0, frame])
                & (key_col < valid_cols[0, frame])
            )
            if frame == left:
                allowed = allowed | (key_cell == lane)
            if frame == right:
                allowed = allowed | (key_cell + TILE == lane)
            start = (OFFSET[pair] + slot) * TILE
            bias[start : start + TILE, :] = jnp.where(allowed, 0.0, -1e30)


def gather_rows(info, scratch, own, other):
    own_start = pl.multiple_of(info[ME] * LOCAL, LOCAL)
    other_start = pl.multiple_of((1 - info[ME]) * LOCAL, LOCAL)
    scratch[pl.ds(own_start, LOCAL), :] = own
    scratch[pl.ds(other_start, LOCAL), :] = other


def probs_kernel(
    info, clips, valid_rows, valid_cols, q_own, k_own, q_other, k_other, slab,
    probs_early, probs_late, slab_out, q_all, k_all, bias, logits_all,
):
    @pl.when(pl.program_id(0) == 0)
    def _():
        fill_bias(clips, valid_rows, valid_cols, bias)

    gather_rows(info, q_all, q_own[...], q_other[0])
    gather_rows(info, k_all, k_own[...], k_other[0])

    def find_logits(pair):
        first, count, offset = FIRST_KEY[pair], KEY_COUNT[pair], OFFSET[pair]
        query = q_all[pair * PAIR : (pair + 1) * PAIR, :]
        score = dot(k_all[first * TILE : (first + count) * TILE, :], query, NT)
        top = None
        for slot in range(count):
            rows = slice(slot * TILE, (slot + 1) * TILE)
            start = (offset + slot) * TILE
            part = score[rows, :] * (SCALE * LOG2E) + bias[start : start + TILE, :]
            logits_all[pair % 2, rows, :] = part
            part = jnp.max(part.reshape(TILE // 8, 8, PAIR), axis=0)
            top = part if top is None else jnp.maximum(top, part)
        return jnp.max(top, axis=0, keepdims=True)

    def find_probs(pair, top, kept):
        count, offset = KEY_COUNT[pair], OFFSET[pair]
        logits = logits_all.at[pair % 2]
        total = None
        for slot in range(count):
            rows = slice(slot * TILE, (slot + 1) * TILE)
            weight = jnp.exp2(logits[rows, :] - top)
            logits[rows, :] = weight
            part = jnp.sum(weight.reshape(TILE // 8, 8, PAIR), axis=0)
            total = part if total is None else total + part
        inverse = 1.0 / jnp.sum(total, axis=0, keepdims=True)
        for slot in range(count):
            rows = slice(slot * TILE, (slot + 1) * TILE)
            start = (offset + slot) * TILE
            kept[start : start + TILE, :] = (logits[rows, :] * inverse).astype(jnp.bfloat16)

    def find_all(kept):
        top = find_logits(0)
        for pair in range(4):
            later = find_logits(pair + 1) if pair < 3 else None
            find_probs(pair, top, kept)
            top = later

    @pl.when(pl.program_id(0) < 4)
    def _():
        find_all(probs_early.at[0])

    @pl.when(pl.program_id(0) >= 4)
    def _():
        find_all(probs_late.at[0])


def probs_call(tables, q, k, others, slab):
    def head_at(step, info):
        return lax.rem(info[MINE] + step, 6)

    def other_block(which):
        return pl.BlockSpec(
            (1, LOCAL, HEAD_DIM), lambda step, info, *_: (which, 0, head_at(step, info))
        )

    own = pl.BlockSpec(
        (LOCAL, HEAD_DIM), lambda step, info, *_: (0, info[ME] * 6 + head_at(step, info))
    )
    block = (1, SLOTS * TILE, PAIR)
    return pl.pallas_call(
        probs_kernel,
        out_shape=[
            jax.ShapeDtypeStruct((4, SLOTS * TILE, PAIR), jnp.bfloat16),
            jax.ShapeDtypeStruct((2, SLOTS * TILE, PAIR), jnp.bfloat16),
            jax.ShapeDtypeStruct(slab.shape, slab.dtype),
        ],
        grid_spec=pltpu.PrefetchScalarGridSpec(
            num_scalar_prefetch=4,
            grid=(6,),
            in_specs=[own, own, other_block(0), other_block(1), pl.BlockSpec(memory_space=pl.ANY)],
            out_specs=[
                pl.BlockSpec(block, lambda step, *_: (jnp.minimum(step, 3), 0, 0)),
                pl.BlockSpec(block, lambda step, *_: (jnp.maximum(step, 4) - 4, 0, 0)),
                pl.BlockSpec(memory_space=pl.ANY),
            ],
            scratch_shapes=[
                pltpu.VMEM((GROUP, HEAD_DIM), jnp.bfloat16),
                pltpu.VMEM((GROUP, HEAD_DIM), jnp.bfloat16),
                pltpu.VMEM((SLOTS * TILE, PAIR), jnp.float32),
                pltpu.VMEM((2, KEY_MOST, PAIR), jnp.float32),
            ],
        ),
        compiler_params=pltpu.CompilerParams(vmem_limit_bytes=VMEM),
        cost_estimate=pl.CostEstimate(
            flops=6 * 2 * SLOTS * TILE * PAIR * HEAD_DIM,
            bytes_accessed=12_000_000,
            transcendentals=6 * SLOTS * TILE * PAIR,
        ),
        input_output_aliases={8: 2},
        name="probs",
    )(*tables, q, k, others, others, slab)


def project(info, valid_rows, valid_cols, grad_all, grad_own, grad_other, weight):
    cell = lax.broadcasted_iota(jnp.int32, (TILE, HEAD_DIM), 0)
    row, col = cell >> 4, cell & (TILE_W - 1)
    for begin, grad_out in ((info[ME] * 4, grad_own), ((1 - info[ME]) * 4, grad_other)):
        grad = dot(grad_out[...], weight, NT)
        for step in range(4):
            frame = begin + step
            valid = (row < valid_rows[0, frame]) & (col < valid_cols[0, frame])
            rows = pl.ds(pl.multiple_of(frame * TILE, TILE), TILE)
            for head in range(2):
                part = grad[step * TILE : (step + 1) * TILE, head * TILE : (head + 1) * TILE]
                grad_all[head, rows, :] = jnp.where(valid, part, 0.0).astype(jnp.bfloat16)


def place_weight(info, pieces, refs, weight):
    for (slab, slots), ref in zip(pieces, refs):
        for index, slot in enumerate(slots):
            chunk = lax.rem(info[INNER] + SLOT_SHIFT[slot], 4)
            start = pl.multiple_of(slab * SLAB + chunk * CHUNK, 16)
            weight[pl.ds(start, CHUNK), :] = ref[index]


def grads_kernel(pieces, row_slot, info, clips, valid_rows, valid_cols, *refs):
    weight_refs, refs = refs[: len(pieces)], refs[len(pieces) :]
    grad_own, grad_other, probs = refs[:3]
    own_heads, other_heads = (refs[3:6], refs[6:9]), (refs[9:12], refs[12:15])
    kept, sent, weight, grad_all, q_all, k_all, v_all, grad_probs_all, grad_scores_all = refs[15:24]
    dq_all, dk_all, dv_all = refs[24:]
    me = info[ME]
    step = pl.program_id(0)
    probs_heads = [probs.at[2 * step + head] for head in range(2)]

    @pl.when(step == 0)
    def _():
        place_weight(info, pieces, weight_refs, weight)

    start = pl.multiple_of(info[row_slot] + step * PAIR, 64)
    rows = weight[pl.ds(start, PAIR), :]
    project(info, valid_rows, valid_cols, grad_all, grad_own, grad_other, rows)
    for head in range(2):
        for scratch, own, other in zip(
            (q_all, k_all, v_all), own_heads[head], other_heads[head]
        ):
            gather_rows(info, scratch.at[head], own[...], other[0])

    def spans(pair):
        first, count = FIRST_KEY[pair], KEY_COUNT[pair]
        key_rows = slice(first * TILE, (first + count) * TILE)
        table_rows = slice(OFFSET[pair] * TILE, (OFFSET[pair] + count) * TILE)
        return key_rows, slice(pair * PAIR, (pair + 1) * PAIR), table_rows, count

    def find_grad_probs(item):
        head, pair = divmod(item, 4)
        key_rows, queries, _, count = spans(pair)
        grad_probs_all[item % 2, : count * TILE, :] = dot(
            v_all[head, key_rows, :], grad_all[head, queries, :], NT
        )

    def find_grad_scores(item):
        head, pair = divmod(item, 4)
        _, _, table_rows, count = spans(pair)
        grad_probs, grad_scores = grad_probs_all.at[item % 2], grad_scores_all.at[item % 2]
        probs = probs_heads[head]
        delta = None
        for slot in range(count):
            rows = slice(slot * TILE, (slot + 1) * TILE)
            start = table_rows.start + slot * TILE
            part = grad_probs[rows, :] * probs[start : start + TILE, :].astype(jnp.float32)
            part = jnp.sum(part.reshape(TILE // 8, 8, PAIR), axis=0)
            delta = part if delta is None else delta + part
        delta = jnp.sum(delta, axis=0, keepdims=True)
        for slot in range(count):
            rows = slice(slot * TILE, (slot + 1) * TILE)
            start = table_rows.start + slot * TILE
            weights = probs[start : start + TILE, :].astype(jnp.float32)
            grad_scores[rows, :] = (weights * (grad_probs[rows, :] - delta)).astype(jnp.bfloat16)

    def add_grads(item):
        head, pair = divmod(item, 4)
        key_rows, queries, table_rows, count = spans(pair)
        scores = grad_scores_all[item % 2, : count * TILE, :]
        dq_all[head, queries, :] = dot(scores, k_all[head, key_rows, :], TN)
        dk_all[head, key_rows, :] += dot(scores, q_all[head, queries, :], NN)
        dv_all[head, key_rows, :] += dot(
            probs_heads[head][table_rows, :], grad_all[head, queries, :], NN
        )

    def hand_over(head):
        cols = slice(head * HEAD_DIM, (head + 1) * HEAD_DIM)
        own = pl.ds(pl.multiple_of(me * LOCAL, LOCAL), LOCAL)
        other = pl.ds(pl.multiple_of((1 - me) * LOCAL, LOCAL), LOCAL)
        for index, (part, scale) in enumerate(((dq_all, SCALE), (dk_all, SCALE), (dv_all, 1.0))):
            kept[index, :, cols] = (part[head, own, :] * scale).astype(jnp.bfloat16)
            sent[index, :, cols] = (part[head, other, :] * scale).astype(jnp.bfloat16)

    dk_all[...] = jnp.zeros_like(dk_all)
    dv_all[...] = jnp.zeros_like(dv_all)
    find_grad_probs(0)
    for item in range(8):
        if item < 7:
            find_grad_probs(item + 1)
        if item > 0:
            add_grads(item - 1)
        find_grad_scores(item)
        if item == 5:
            hand_over(0)
    add_grads(7)
    hand_over(1)


def grads_call(tables, pieces, begin, heads, row_slot, tokens, probs):
    def head_at(parity, step, info):
        return lax.rem(info[MINE] + begin + 2 * step + parity, 6)

    def own_block(parity):
        return pl.BlockSpec(
            (LOCAL, HEAD_DIM),
            lambda step, info, *_: (0, info[ME] * 6 + head_at(parity, step, info)),
        )

    def other_block(parity, which):
        return pl.BlockSpec(
            (1, LOCAL, HEAD_DIM),
            lambda step, info, *_: (which, 0, head_at(parity, step, info)),
        )

    whole = pl.BlockSpec(memory_space=pltpu.VMEM)
    result = jax.ShapeDtypeStruct((3, LOCAL, heads * HEAD_DIM), jnp.bfloat16)
    arrays = [piece for _, _, piece in pieces]
    layout = tuple((slab, slots) for slab, slots, _ in pieces)
    grad_own, grad_other, *own, other = tokens
    return pl.pallas_call(
        functools.partial(grads_kernel, layout, row_slot),
        out_shape=[result] * 2,
        grid_spec=pltpu.PrefetchScalarGridSpec(
            num_scalar_prefetch=4,
            grid=(heads // 2,),
            in_specs=[whole] * (len(arrays) + 3)
            + [own_block(parity) for parity in range(2) for _ in range(3)]
            + [other_block(parity, which) for parity in range(2) for which in range(3)],
            out_specs=[pl.BlockSpec((3, LOCAL, PAIR), lambda step, *_: (0, 0, step))] * 2,
            scratch_shapes=[
                pltpu.VMEM((3 * SLAB, DIM), jnp.bfloat16),
                pltpu.VMEM((2, GROUP, HEAD_DIM), jnp.bfloat16),
                pltpu.VMEM((2, GROUP, HEAD_DIM), jnp.bfloat16),
                pltpu.VMEM((2, GROUP, HEAD_DIM), jnp.bfloat16),
                pltpu.VMEM((2, GROUP, HEAD_DIM), jnp.bfloat16),
                pltpu.VMEM((2, KEY_MOST, PAIR), jnp.float32),
                pltpu.VMEM((2, KEY_MOST, PAIR), jnp.bfloat16),
                pltpu.VMEM((2, GROUP, HEAD_DIM), jnp.float32),
                pltpu.VMEM((2, GROUP, HEAD_DIM), jnp.float32),
                pltpu.VMEM((2, GROUP, HEAD_DIM), jnp.float32),
            ],
        ),
        compiler_params=pltpu.CompilerParams(vmem_limit_bytes=VMEM),
        cost_estimate=pl.CostEstimate(
            flops=heads * (8 * SLOTS * TILE * PAIR * HEAD_DIM + 2 * GROUP * HEAD_DIM * DIM),
            bytes_accessed=5_000_000 * heads,
            transcendentals=0,
        ),
        name="grads",
    )(*tables, *arrays, grad_own, grad_other, probs, *own, *own, *[other] * 6)


def merge_kernel(plan, count, info, *refs):
    parts, outs, sems = refs[count : count + len(plan)], refs[-4:-1], refs[-1]
    copies = []
    for part, (theirs, begin, heads) in zip(parts, plan):
        core, first = (1 - info[ME], info[THEIRS]) if theirs else (info[ME], info[MINE])
        for step in range(heads):
            head = core * 6 + lax.rem(first + begin + step, 6)
            cols = pl.ds(pl.multiple_of(head * HEAD_DIM, HEAD_DIM), HEAD_DIM)
            for index, out in enumerate(outs):
                copies.append(
                    pltpu.make_async_copy(
                        part.at[index, :, step * HEAD_DIM : (step + 1) * HEAD_DIM],
                        out.at[:, cols],
                        sems.at[len(copies)],
                    )
                )
    for copy in copies:
        copy.start()
    for copy in copies:
        copy.wait()


def merge_call(info, earlier, parts):
    full = jax.ShapeDtypeStruct((LOCAL, WIDTH), jnp.bfloat16)
    plan = tuple(part[:3] for part in parts)
    copies = sum(3 * heads for _, _, heads in plan)
    return pl.pallas_call(
        functools.partial(merge_kernel, plan, len(earlier)),
        out_shape=[full] * 3,
        grid_spec=pltpu.PrefetchScalarGridSpec(
            num_scalar_prefetch=1,
            grid=(1,),
            in_specs=[pl.BlockSpec(memory_space=pl.ANY)] * len(earlier)
            + [pl.BlockSpec(memory_space=pltpu.VMEM)] * len(parts),
            out_specs=[pl.BlockSpec(memory_space=pl.ANY)] * 3,
            scratch_shapes=[pltpu.SemaphoreType.DMA((copies,))],
        ),
        input_output_aliases={1 + i: i for i in range(len(earlier))},
        compiler_params=pltpu.CompilerParams(vmem_limit_bytes=VMEM),
        name="merge",
    )(info, *earlier, *[part[3] for part in parts])


def place_table():
    table = np.zeros((NZ * NY * NX, 2, 6), np.int32)
    for dp in range(NZ * NY * NX):
        y, quarter = dp // NX % NY, dp // (NY * NX) % 4
        for core in range(2):
            outer, inner = (y, quarter) if core == 0 else (quarter, y)
            begin = (5, 0, 2, 3)
            rows = 64 * (1 - outer % 2)
            table[dp, core] = (core, begin[outer], begin[inner], inner, rows, 128 + rows)
    return table.reshape(-1, 6)


def place(z, y, x, core):
    return (((z % NZ) * NY + y % NY) * NX + x % NX) * 2 + core


def move(value, source):
    places = [
        (z, y, x, core) for z in range(NZ) for y in range(NY) for x in range(NX) for core in range(2)
    ]
    pairs = [(source(*taker), place(*taker)) for taker in places]
    return lax.ppermute(value, ("dp", "frame"), pairs)


def first_rows(step):
    def source(z, y, x, core):
        inner, outer = (z % 4, y) if core == 0 else (y, z % 4)
        return 128 * core + 8 * (4 * outer + inner) + 2 * x + ((z // 4) ^ step)

    return source


def along(last, distance):
    def source(z, y, x, core):
        if (core == 0) == last:
            return place(z, y + distance, x, core)
        return place(z + distance, y, x, core)

    return source


def line_rows(out_weight, z):
    x_lines = [
        [(z * NY + y) * NX + x for x in range(NX)] for z in range(NZ) for y in range(NY)
    ]
    even, odd = (move(out_weight, first_rows(step)) for step in range(2))
    rows = jnp.stack([jnp.where(z >= 4, odd, even), jnp.where(z >= 4, even, odd)])
    return lax.all_to_all(
        jnp.broadcast_to(rows[None], (NX,) + rows.shape),
        "dp",
        0,
        0,
        axis_index_groups=x_lines,
        tiled=True,
    ).reshape(1, CHUNK, DIM)


def beside_rows(rows):
    return [move(rows, along(False, distance)) for distance in (1, -1, 2)]


def far_slab(after_low, before_high):
    return move(after_low, along(True, 1)), move(before_high, along(True, -1))


def swap(value):
    return lax.ppermute(value, "frame", [(0, 1), (1, 0)])


def other_half(value, me):
    return jnp.where(me == 0, value[:, HALF:], value[:, :HALF])


def on_device(queries, keys, values, grad_out, out_weight, frame_clip, frame_rows, frame_cols):
    me = lax.axis_index("frame")
    dp = lax.axis_index("dp")
    info = lax.dynamic_index_in_dim(jnp.asarray(place_table()), dp * 2 + me, 0, keepdims=False)
    tables = (info, frame_clip, frame_rows, frame_cols)
    g_other = swap(grad_out)
    others = swap(jnp.stack([other_half(x, me) for x in (queries, keys, values)]))
    rows = line_rows(out_weight, dp // (NY * NX))
    slab = jnp.concatenate([rows] + beside_rows(rows))
    after_low, before_high = move(slab[:2], along(True, 1)), move(slab[2:], along(True, -1))
    probs_early, probs_late, slab = probs_call(tables, queries, keys, others, slab)
    after_high, before_low = move(slab[2:], along(True, 1)), move(slab[:2], along(True, -1))
    far_low, far_high = far_slab(after_low, before_high)
    tokens = (grad_out, g_other, queries, keys, values, others)
    low, high, both = (0, 1), (2, 3), (0, 1, 2, 3)
    pieces = (
        (0, low, before_low),
        (0, high, before_high),
        (1, both, slab),
        (2, low, after_low),
        (2, high, after_high),
    )
    kept, sent = grads_call(tables, pieces, 0, 4, ROWS_EARLY, tokens, probs_early)
    arrived = swap(sent)
    pieces = (
        (0, low, after_low),
        (0, high, after_high),
        (1, low, far_low),
        (1, high, far_high),
        (2, low, before_low),
        (2, high, before_high),
    )
    kept_late, sent_late = grads_call(tables, pieces, 4, 2, ROWS_LATE, tokens, probs_late)
    arrived_late = swap(sent_late)
    parts = ((False, 0, 4, kept), (False, 4, 2, kept_late), (True, 0, 4, arrived))
    outs = merge_call(info, (), parts)
    return tuple(merge_call(info, tuple(outs), ((True, 4, 2, arrived_late),)))


def solution(mesh):
    split = P(("dp", "frame"), None)
    table = P("dp", None)
    return jax.shard_map(
        on_device,
        mesh=mesh,
        in_specs=(split,) * 5 + (table,) * 3,
        out_specs=(split,) * 3,
        check_vma=False,
    )
```

```python
import functools

import jax
import jax.numpy as jnp
import numpy as np
from jax import lax
from jax.experimental import pallas as pl
from jax.experimental.pallas import tpu as pltpu
from jax.sharding import PartitionSpec as P

HEAD_DIM = 128
TILE_W = 16
TILE = 128
RADIUS = 3
FRAMES = 8
LOCAL = 512
GROUP = 1024
HALF = 768
WIDTH = 1536
DIM = 3072
PAIR = 2 * TILE
SCALE = 1.0 / HEAD_DIM**0.5
LOG2E = 1.4426950408889634

FIRST_KEY = (0, 0, 1, 3)
KEY_COUNT = (5, 7, 7, 5)
OFFSET = (0, 5, 12, 19)
SLOTS = 24
KEY_MOST = 7 * TILE
VMEM = 26 * 1024 * 1024

CHUNK = 48
SLAB = 192
NZ, NY, NX = 8, 4, 4
SLOT_SHIFT = (0, 1, 3, 2)
ME, MINE, THEIRS, INNER, ROWS_EARLY, ROWS_LATE = range(6)

NT = (((1,), (1,)), ((), ()))
TN = (((0,), (0,)), ((), ()))
NN = (((1,), (0,)), ((), ()))


def dot(lhs, rhs, dims):
    return lax.dot_general(lhs, rhs, dims, preferred_element_type=jnp.float32)


def fill_bias(clips, valid_rows, valid_cols, bias):
    key_cell = lax.broadcasted_iota(jnp.int32, (TILE, PAIR), 0)
    lane = lax.broadcasted_iota(jnp.int32, (TILE, PAIR), 1)
    query_cell = lane & (TILE - 1)
    key_row, key_col = key_cell >> 4, key_cell & (TILE_W - 1)
    near = (jnp.abs(key_row - (query_cell >> 4)) <= RADIUS) & (
        jnp.abs(key_col - (query_cell & (TILE_W - 1))) <= RADIUS
    )
    second = lane >= TILE
    for pair in range(4):
        left, right = 2 * pair, 2 * pair + 1
        for slot in range(KEY_COUNT[pair]):
            frame = FIRST_KEY[pair] + slot
            clip = clips[0, frame]
            left_same = (clips[0, left] == clip) & (abs(frame - left) <= RADIUS)
            right_same = (clips[0, right] == clip) & (abs(frame - right) <= RADIUS)
            linked = jnp.where(
                second, right_same.astype(jnp.int32), left_same.astype(jnp.int32)
            )
            allowed = (
                near
                & (linked > 0)
                & (key_row < valid_rows[0, frame])
                & (key_col < valid_cols[0, frame])
            )
            if frame == left:
                allowed = allowed | (key_cell == lane)
            if frame == right:
                allowed = allowed | (key_cell + TILE == lane)
            start = (OFFSET[pair] + slot) * TILE
            bias[start : start + TILE, :] = jnp.where(allowed, 0.0, -1e30)


def gather_rows(info, scratch, own, other):
    own_start = pl.multiple_of(info[ME] * LOCAL, LOCAL)
    other_start = pl.multiple_of((1 - info[ME]) * LOCAL, LOCAL)
    scratch[pl.ds(own_start, LOCAL), :] = own
    scratch[pl.ds(other_start, LOCAL), :] = other


def probs_kernel(
    passing, loading, info, clips, valid_rows, valid_cols, q_own, k_own, q_other, k_other, *refs
):
    loads, refs = refs[:loading], refs[loading + passing :]
    kept = refs[0].at[0]
    loaded, refs = refs[1 : 1 + loading // 2], refs[1 + loading // 2 + passing :]
    q_all, k_all, bias, logits_all = refs[:4]
    step = pl.program_id(0)
    copies = []
    for index, part in enumerate(loads):
        core = (info[ME], 1 - info[ME])[index]
        rows = pl.ds(pl.multiple_of(core * LOCAL, LOCAL), LOCAL)
        copies.append(pltpu.make_async_copy(part, loaded[0].at[rows, :], refs[4].at[index]))

    @pl.when(step == 0)
    def _():
        for copy in copies:
            copy.start()

    @pl.when(pl.program_id(0) == 0)
    def _():
        fill_bias(clips, valid_rows, valid_cols, bias)

    gather_rows(info, q_all, q_own[...], q_other[0])
    gather_rows(info, k_all, k_own[...], k_other[0])

    def find_logits(pair):
        first, count, offset = FIRST_KEY[pair], KEY_COUNT[pair], OFFSET[pair]
        query = q_all[pair * PAIR : (pair + 1) * PAIR, :]
        score = dot(k_all[first * TILE : (first + count) * TILE, :], query, NT)
        top = None
        for slot in range(count):
            rows = slice(slot * TILE, (slot + 1) * TILE)
            start = (offset + slot) * TILE
            part = score[rows, :] * (SCALE * LOG2E) + bias[start : start + TILE, :]
            logits_all[pair % 2, rows, :] = part
            part = jnp.max(part.reshape(TILE // 8, 8, PAIR), axis=0)
            top = part if top is None else jnp.maximum(top, part)
        return jnp.max(top, axis=0, keepdims=True)

    def find_probs(pair, top):
        count, offset = KEY_COUNT[pair], OFFSET[pair]
        logits = logits_all.at[pair % 2]
        total = None
        for slot in range(count):
            rows = slice(slot * TILE, (slot + 1) * TILE)
            weight = jnp.exp2(logits[rows, :] - top)
            logits[rows, :] = weight
            part = jnp.sum(weight.reshape(TILE // 8, 8, PAIR), axis=0)
            total = part if total is None else total + part
        inverse = 1.0 / jnp.sum(total, axis=0, keepdims=True)
        for slot in range(count):
            rows = slice(slot * TILE, (slot + 1) * TILE)
            start = (offset + slot) * TILE
            kept[start : start + TILE, :] = (logits[rows, :] * inverse).astype(jnp.bfloat16)

    top = find_logits(0)
    for pair in range(4):
        later = find_logits(pair + 1) if pair < 3 else None
        find_probs(pair, top)
        top = later

    @pl.when(step == pl.num_programs(0) - 1)
    def _():
        for copy in copies:
            copy.wait()


def probs_call(tables, q, k, others, begin, heads, passing, loads=()):
    def head_at(step, info):
        return lax.rem(info[MINE] + begin + step, 6)

    def other_block(which):
        return pl.BlockSpec(
            (1, LOCAL, HEAD_DIM), lambda step, info, *_: (which, 0, head_at(step, info))
        )

    own = pl.BlockSpec(
        (LOCAL, HEAD_DIM), lambda step, info, *_: (0, info[ME] * 6 + head_at(step, info))
    )
    block = (1, SLOTS * TILE, PAIR)
    anywhere = pl.BlockSpec(memory_space=pl.ANY)
    loaded = [jax.ShapeDtypeStruct((GROUP, DIM), jnp.bfloat16)] * (len(loads) // 2)
    return pl.pallas_call(
        functools.partial(probs_kernel, len(passing), len(loads)),
        out_shape=[jax.ShapeDtypeStruct((heads, SLOTS * TILE, PAIR), jnp.bfloat16)]
        + loaded
        + [jax.ShapeDtypeStruct(x.shape, x.dtype) for x in passing],
        grid_spec=pltpu.PrefetchScalarGridSpec(
            num_scalar_prefetch=4,
            grid=(heads,),
            in_specs=[own, own, other_block(0), other_block(1)]
            + [pl.BlockSpec(memory_space=pl.ANY)] * len(loads)
            + [anywhere] * len(passing),
            out_specs=[pl.BlockSpec(block, lambda step, *_: (step, 0, 0))]
            + [pl.BlockSpec(memory_space=pltpu.VMEM)] * len(loaded)
            + [anywhere] * len(passing),
            scratch_shapes=[
                pltpu.VMEM((GROUP, HEAD_DIM), jnp.bfloat16),
                pltpu.VMEM((GROUP, HEAD_DIM), jnp.bfloat16),
                pltpu.VMEM((SLOTS * TILE, PAIR), jnp.float32),
                pltpu.VMEM((2, KEY_MOST, PAIR), jnp.float32),
                pltpu.SemaphoreType.DMA((2,)),
            ],
        ),
        compiler_params=pltpu.CompilerParams(vmem_limit_bytes=VMEM),
        cost_estimate=pl.CostEstimate(
            flops=heads * 2 * SLOTS * TILE * PAIR * HEAD_DIM,
            bytes_accessed=2_000_000 * heads,
            transcendentals=heads * SLOTS * TILE * PAIR,
        ),
        input_output_aliases={
            8 + len(loads) + i: 1 + len(loaded) + i for i in range(len(passing))
        },
        name="probs",
    )(*tables, q, k, others, others, *loads, *passing)


def project(valid_rows, valid_cols, grad_all, grad_out, weight):
    cell = lax.broadcasted_iota(jnp.int32, (TILE, HEAD_DIM), 0)
    row, col = cell >> 4, cell & (TILE_W - 1)
    for half in range(2):
        grad = dot(grad_out[half * LOCAL : (half + 1) * LOCAL, :], weight, NT)
        for step in range(4):
            frame = half * 4 + step
            valid = (row < valid_rows[0, frame]) & (col < valid_cols[0, frame])
            rows = slice(frame * TILE, (frame + 1) * TILE)
            for head in range(2):
                part = grad[step * TILE : (step + 1) * TILE, head * TILE : (head + 1) * TILE]
                grad_all[head, rows, :] = jnp.where(valid, part, 0.0).astype(jnp.bfloat16)


def place_weight(info, pieces, refs, weight):
    for (slab, slots), ref in zip(pieces, refs):
        for index, slot in enumerate(slots):
            chunk = lax.rem(info[INNER] + SLOT_SHIFT[slot], 4)
            start = pl.multiple_of(slab * SLAB + chunk * CHUNK, 16)
            weight[pl.ds(start, CHUNK), :] = ref[index]


def grads_kernel(pieces, row_slot, info, clips, valid_rows, valid_cols, *refs):
    weight_refs, refs = refs[: len(pieces)], refs[len(pieces) :]
    grad_out, probs = refs[:2]
    own_heads, other_heads = (refs[2:5], refs[5:8]), (refs[8:11], refs[11:14])
    kept, sent, weight, grad_all, q_all, k_all, v_all, grad_probs_all, grad_scores_all = refs[14:23]
    dq_all, dk_all, dv_all = refs[23:]
    me = info[ME]
    step = pl.program_id(0)
    probs_heads = [probs.at[2 * step + head] for head in range(2)]

    @pl.when(step == 0)
    def _():
        place_weight(info, pieces, weight_refs, weight)

    start = pl.multiple_of(info[row_slot] + step * PAIR, 64)
    rows = weight[pl.ds(start, PAIR), :]
    project(valid_rows, valid_cols, grad_all, grad_out, rows)
    for head in range(2):
        for scratch, own, other in zip(
            (q_all, k_all, v_all), own_heads[head], other_heads[head]
        ):
            gather_rows(info, scratch.at[head], own[...], other[0])

    def spans(pair):
        first, count = FIRST_KEY[pair], KEY_COUNT[pair]
        key_rows = slice(first * TILE, (first + count) * TILE)
        table_rows = slice(OFFSET[pair] * TILE, (OFFSET[pair] + count) * TILE)
        return key_rows, slice(pair * PAIR, (pair + 1) * PAIR), table_rows, count

    def find_grad_probs(item):
        head, pair = divmod(item, 4)
        key_rows, queries, _, count = spans(pair)
        grad_probs_all[item % 2, : count * TILE, :] = dot(
            v_all[head, key_rows, :], grad_all[head, queries, :], NT
        )

    def find_grad_scores(item):
        head, pair = divmod(item, 4)
        _, _, table_rows, count = spans(pair)
        grad_probs, grad_scores = grad_probs_all.at[item % 2], grad_scores_all.at[item % 2]
        probs = probs_heads[head]
        delta = None
        for slot in range(count):
            rows = slice(slot * TILE, (slot + 1) * TILE)
            start = table_rows.start + slot * TILE
            part = grad_probs[rows, :] * probs[start : start + TILE, :].astype(jnp.float32)
            part = jnp.sum(part.reshape(TILE // 8, 8, PAIR), axis=0)
            delta = part if delta is None else delta + part
        delta = jnp.sum(delta, axis=0, keepdims=True)
        for slot in range(count):
            rows = slice(slot * TILE, (slot + 1) * TILE)
            start = table_rows.start + slot * TILE
            weights = probs[start : start + TILE, :].astype(jnp.float32)
            grad_scores[rows, :] = (weights * (grad_probs[rows, :] - delta)).astype(jnp.bfloat16)

    def add_grads(item):
        head, pair = divmod(item, 4)
        key_rows, queries, table_rows, count = spans(pair)
        scores = grad_scores_all[item % 2, : count * TILE, :]
        dq_all[head, queries, :] = dot(scores, k_all[head, key_rows, :], TN)
        dk_all[head, key_rows, :] += dot(scores, q_all[head, queries, :], NN)
        dv_all[head, key_rows, :] += dot(
            probs_heads[head][table_rows, :], grad_all[head, queries, :], NN
        )

    def hand_over(head):
        cols = slice(head * HEAD_DIM, (head + 1) * HEAD_DIM)
        own = pl.ds(pl.multiple_of(me * LOCAL, LOCAL), LOCAL)
        other = pl.ds(pl.multiple_of((1 - me) * LOCAL, LOCAL), LOCAL)
        for index, (part, scale) in enumerate(((dq_all, SCALE), (dk_all, SCALE), (dv_all, 1.0))):
            kept[index, :, cols] = (part[head, own, :] * scale).astype(jnp.bfloat16)
            sent[index, :, cols] = (part[head, other, :] * scale).astype(jnp.bfloat16)

    dk_all[...] = jnp.zeros_like(dk_all)
    dv_all[...] = jnp.zeros_like(dv_all)
    find_grad_probs(0)
    for item in range(8):
        if item < 7:
            find_grad_probs(item + 1)
        if item > 0:
            add_grads(item - 1)
        find_grad_scores(item)
        if item == 5:
            hand_over(0)
    add_grads(7)
    hand_over(1)


def grads_call(tables, pieces, begin, heads, row_slot, tokens, probs):
    def head_at(parity, step, info):
        return lax.rem(info[MINE] + begin + 2 * step + parity, 6)

    def own_block(parity):
        return pl.BlockSpec(
            (LOCAL, HEAD_DIM),
            lambda step, info, *_: (0, info[ME] * 6 + head_at(parity, step, info)),
        )

    def other_block(parity, which):
        return pl.BlockSpec(
            (1, LOCAL, HEAD_DIM),
            lambda step, info, *_: (which, 0, head_at(parity, step, info)),
        )

    whole = pl.BlockSpec(memory_space=pltpu.VMEM)
    result = jax.ShapeDtypeStruct((3, LOCAL, heads * HEAD_DIM), jnp.bfloat16)
    arrays = [piece for _, _, piece in pieces]
    layout = tuple((slab, slots) for slab, slots, _ in pieces)
    grad_out, *own, other = tokens
    return pl.pallas_call(
        functools.partial(grads_kernel, layout, row_slot),
        out_shape=[result] * 2,
        grid_spec=pltpu.PrefetchScalarGridSpec(
            num_scalar_prefetch=4,
            grid=(heads // 2,),
            in_specs=[whole] * (len(arrays) + 2)
            + [own_block(parity) for parity in range(2) for _ in range(3)]
            + [other_block(parity, which) for parity in range(2) for which in range(3)],
            out_specs=[pl.BlockSpec((3, LOCAL, PAIR), lambda step, *_: (0, 0, step))] * 2,
            scratch_shapes=[
                pltpu.VMEM((3 * SLAB, DIM), jnp.bfloat16),
                pltpu.VMEM((2, GROUP, HEAD_DIM), jnp.bfloat16),
                pltpu.VMEM((2, GROUP, HEAD_DIM), jnp.bfloat16),
                pltpu.VMEM((2, GROUP, HEAD_DIM), jnp.bfloat16),
                pltpu.VMEM((2, GROUP, HEAD_DIM), jnp.bfloat16),
                pltpu.VMEM((2, KEY_MOST, PAIR), jnp.float32),
                pltpu.VMEM((2, KEY_MOST, PAIR), jnp.bfloat16),
                pltpu.VMEM((2, GROUP, HEAD_DIM), jnp.float32),
                pltpu.VMEM((2, GROUP, HEAD_DIM), jnp.float32),
                pltpu.VMEM((2, GROUP, HEAD_DIM), jnp.float32),
            ],
        ),
        compiler_params=pltpu.CompilerParams(vmem_limit_bytes=VMEM),
        cost_estimate=pl.CostEstimate(
            flops=heads * (8 * SLOTS * TILE * PAIR * HEAD_DIM + 2 * GROUP * HEAD_DIM * DIM),
            bytes_accessed=5_000_000 * heads,
            transcendentals=0,
        ),
        name="grads",
    )(*tables, *arrays, grad_out, probs, *own, *own, *[other] * 6)


def merge_kernel(plan, count, info, *refs):
    parts, outs, sems = refs[count : count + len(plan)], refs[-4:-1], refs[-1]
    copies = []
    for part, (theirs, begin, heads) in zip(parts, plan):
        core, first = (1 - info[ME], info[THEIRS]) if theirs else (info[ME], info[MINE])
        for step in range(heads):
            head = core * 6 + lax.rem(first + begin + step, 6)
            cols = pl.ds(pl.multiple_of(head * HEAD_DIM, HEAD_DIM), HEAD_DIM)
            for index, out in enumerate(outs):
                copies.append(
                    pltpu.make_async_copy(
                        part.at[index, :, step * HEAD_DIM : (step + 1) * HEAD_DIM],
                        out.at[:, cols],
                        sems.at[len(copies)],
                    )
                )
    for copy in copies:
        copy.start()
    for copy in copies:
        copy.wait()


def merge_call(info, earlier, parts):
    full = jax.ShapeDtypeStruct((LOCAL, WIDTH), jnp.bfloat16)
    plan = tuple(part[:3] for part in parts)
    copies = sum(3 * heads for _, _, heads in plan)
    return pl.pallas_call(
        functools.partial(merge_kernel, plan, len(earlier)),
        out_shape=[full] * 3,
        grid_spec=pltpu.PrefetchScalarGridSpec(
            num_scalar_prefetch=1,
            grid=(1,),
            in_specs=[pl.BlockSpec(memory_space=pl.ANY)] * len(earlier)
            + [pl.BlockSpec(memory_space=pltpu.VMEM)] * len(parts),
            out_specs=[pl.BlockSpec(memory_space=pl.ANY)] * 3,
            scratch_shapes=[pltpu.SemaphoreType.DMA((copies,))],
        ),
        input_output_aliases={1 + i: i for i in range(len(earlier))},
        compiler_params=pltpu.CompilerParams(vmem_limit_bytes=VMEM),
        name="merge",
    )(info, *earlier, *[part[3] for part in parts])


def place_table():
    table = np.zeros((NZ * NY * NX, 2, 6), np.int32)
    for dp in range(NZ * NY * NX):
        y, quarter = dp // NX % NY, dp // (NY * NX) % 4
        for core in range(2):
            outer, inner = (y, quarter) if core == 0 else (quarter, y)
            begin = (5, 0, 2, 3)
            rows = 64 * (1 - outer % 2)
            table[dp, core] = (core, begin[outer], begin[inner], inner, rows, 128 + rows)
    return table.reshape(-1, 6)


def place(z, y, x, core):
    return (((z % NZ) * NY + y % NY) * NX + x % NX) * 2 + core


def move(value, source):
    places = [
        (z, y, x, core) for z in range(NZ) for y in range(NY) for x in range(NX) for core in range(2)
    ]
    pairs = [(source(*taker), place(*taker)) for taker in places]
    return lax.ppermute(value, ("dp", "frame"), pairs)


def first_rows(step):
    def source(z, y, x, core):
        inner, outer = (z % 4, y) if core == 0 else (y, z % 4)
        return 128 * core + 8 * (4 * outer + inner) + 2 * x + ((z // 4) ^ step)

    return source


def along(last, distance):
    def source(z, y, x, core):
        if (core == 0) == last:
            return place(z, y + distance, x, core)
        return place(z + distance, y, x, core)

    return source


def line_rows(out_weight, z):
    x_lines = [
        [(z * NY + y) * NX + x for x in range(NX)] for z in range(NZ) for y in range(NY)
    ]
    even, odd = (move(out_weight, first_rows(step)) for step in range(2))
    rows = jnp.stack([jnp.where(z >= 4, odd, even), jnp.where(z >= 4, even, odd)])
    return lax.all_to_all(
        jnp.broadcast_to(rows[None], (NX,) + rows.shape),
        "dp",
        0,
        0,
        axis_index_groups=x_lines,
        tiled=True,
    ).reshape(1, CHUNK, DIM)


def beside_rows(rows):
    return [move(rows, along(False, distance)) for distance in (1, -1, 2)]


def far_slab(after_low, before_high):
    return move(after_low, along(True, 1)), move(before_high, along(True, -1))


def swap(value):
    return lax.ppermute(value, "frame", [(0, 1), (1, 0)])


def halves_kernel(info, *refs):
    values, out, sems = refs[:3], refs[3], refs[4]
    cols = pl.ds(pl.multiple_of((1 - info[ME]) * HALF, HALF), HALF)
    copies = [
        pltpu.make_async_copy(value.at[:, cols], out.at[index], sems.at[index])
        for index, value in enumerate(values)
    ]
    for copy in copies:
        copy.start()
    for copy in copies:
        copy.wait()


def other_halves(info, values):
    return pl.pallas_call(
        halves_kernel,
        out_shape=jax.ShapeDtypeStruct((3, LOCAL, HALF), jnp.bfloat16),
        grid_spec=pltpu.PrefetchScalarGridSpec(
            num_scalar_prefetch=1,
            grid=(1,),
            in_specs=[pl.BlockSpec(memory_space=pl.ANY)] * 3,
            out_specs=pl.BlockSpec(memory_space=pltpu.VMEM),
            scratch_shapes=[pltpu.SemaphoreType.DMA((3,))],
        ),
        compiler_params=pltpu.CompilerParams(vmem_limit_bytes=60 * 1024 * 1024),
        name="halves",
    )(info, *values)


def on_device(queries, keys, values, grad_out, out_weight, frame_clip, frame_rows, frame_cols):
    me = lax.axis_index("frame")
    dp = lax.axis_index("dp")
    info = lax.dynamic_index_in_dim(jnp.asarray(place_table()), dp * 2 + me, 0, keepdims=False)
    tables = (info, frame_clip, frame_rows, frame_cols)
    g_other = swap(grad_out)
    others = swap(other_halves(info, (queries, keys, values)))
    rows = line_rows(out_weight, dp // (NY * NX))
    slab = jnp.concatenate([rows] + beside_rows(rows))
    after_low, before_high = move(slab[:2], along(True, 1)), move(slab[2:], along(True, -1))
    attend = functools.partial(probs_call, tables, queries, keys, others)
    probs_early, g_all, slab = attend(0, 4, (slab,), (grad_out, g_other))
    after_high, before_low = move(slab[2:], along(True, 1)), move(slab[:2], along(True, -1))
    probs_late, after_low, before_high = attend(4, 2, (after_low, before_high))
    far_low, far_high = far_slab(after_low, before_high)
    tokens = (g_all, queries, keys, values, others)
    low, high, both = (0, 1), (2, 3), (0, 1, 2, 3)
    pieces = (
        (0, low, before_low),
        (0, high, before_high),
        (1, both, slab),
        (2, low, after_low),
        (2, high, after_high),
    )
    kept, sent = grads_call(tables, pieces, 0, 4, ROWS_EARLY, tokens, probs_early)
    arrived = swap(sent)
    pieces = (
        (0, low, after_low),
        (0, high, after_high),
        (1, low, far_low),
        (1, high, far_high),
        (2, low, before_low),
        (2, high, before_high),
    )
    kept_late, sent_late = grads_call(tables, pieces, 4, 2, ROWS_LATE, tokens, probs_late)
    arrived_late = swap(sent_late)
    parts = ((False, 0, 4, kept), (False, 4, 2, kept_late), (True, 0, 4, arrived))
    outs = merge_call(info, (), parts)
    return tuple(merge_call(info, tuple(outs), ((True, 4, 2, arrived_late),)))


def solution(mesh):
    split = P(("dp", "frame"), None)
    table = P("dp", None)
    return jax.shard_map(
        on_device,
        mesh=mesh,
        in_specs=(split,) * 5 + (table,) * 3,
        out_specs=(split,) * 3,
        check_vma=False,
    )
```

```python
import functools

import jax
import jax.numpy as jnp
import numpy as np
from jax import lax
from jax.experimental import pallas as pl
from jax.experimental.pallas import tpu as pltpu
from jax.sharding import PartitionSpec as P

HEAD_DIM = 128
TILE_W = 16
TILE = 128
RADIUS = 3
FRAMES = 8
LOCAL = 512
GROUP = 1024
HALF = 768
WIDTH = 1536
DIM = 3072
PAIR = 2 * TILE
SCALE = 1.0 / HEAD_DIM**0.5
LOG2E = 1.4426950408889634

FIRST_KEY = (0, 0, 1, 3)
KEY_COUNT = (5, 7, 7, 5)
OFFSET = (0, 5, 12, 19)
SLOTS = 24
KEY_MOST = 7 * TILE
VMEM = 26 * 1024 * 1024

CHUNK = 48
SLAB = 192
NZ, NY, NX = 8, 4, 4
SLOT_SHIFT = (0, 1, 3, 2)
ME, MINE, THEIRS, INNER, ROWS_EARLY, ROWS_LATE = range(6)

NT = (((1,), (1,)), ((), ()))
TN = (((0,), (0,)), ((), ()))
NN = (((1,), (0,)), ((), ()))


def dot(lhs, rhs, dims):
    return lax.dot_general(lhs, rhs, dims, preferred_element_type=jnp.float32)


def fill_bias(clips, valid_rows, valid_cols, bias):
    key_cell = lax.broadcasted_iota(jnp.int32, (TILE, PAIR), 0)
    lane = lax.broadcasted_iota(jnp.int32, (TILE, PAIR), 1)
    query_cell = lane & (TILE - 1)
    key_row, key_col = key_cell >> 4, key_cell & (TILE_W - 1)
    near = (jnp.abs(key_row - (query_cell >> 4)) <= RADIUS) & (
        jnp.abs(key_col - (query_cell & (TILE_W - 1))) <= RADIUS
    )
    second = lane >= TILE
    for pair in range(4):
        left, right = 2 * pair, 2 * pair + 1
        for slot in range(KEY_COUNT[pair]):
            frame = FIRST_KEY[pair] + slot
            clip = clips[0, frame]
            left_same = (clips[0, left] == clip) & (abs(frame - left) <= RADIUS)
            right_same = (clips[0, right] == clip) & (abs(frame - right) <= RADIUS)
            linked = jnp.where(
                second, right_same.astype(jnp.int32), left_same.astype(jnp.int32)
            )
            allowed = (
                near
                & (linked > 0)
                & (key_row < valid_rows[0, frame])
                & (key_col < valid_cols[0, frame])
            )
            if frame == left:
                allowed = allowed | (key_cell == lane)
            if frame == right:
                allowed = allowed | (key_cell + TILE == lane)
            start = (OFFSET[pair] + slot) * TILE
            bias[start : start + TILE, :] = jnp.where(allowed, 0.0, -1e30)


def gather_rows(info, scratch, own, other):
    own_start = pl.multiple_of(info[ME] * LOCAL, LOCAL)
    other_start = pl.multiple_of((1 - info[ME]) * LOCAL, LOCAL)
    scratch[pl.ds(own_start, LOCAL), :] = own
    scratch[pl.ds(other_start, LOCAL), :] = other


def probs_kernel(
    passing, loading, info, clips, valid_rows, valid_cols, q_own, k_own, q_other, k_other, *refs
):
    loads, refs = refs[:loading], refs[loading + passing :]
    kept = refs[0].at[0]
    loaded, refs = refs[1 : 1 + loading // 2], refs[1 + loading // 2 + passing :]
    q_all, k_all, bias, logits_all = refs[:4]
    step = pl.program_id(0)
    copies = []
    for index, part in enumerate(loads):
        core = (info[ME], 1 - info[ME])[index]
        rows = pl.ds(pl.multiple_of(core * LOCAL, LOCAL), LOCAL)
        copies.append(pltpu.make_async_copy(part, loaded[0].at[rows, :], refs[4].at[index]))

    @pl.when(step == 0)
    def _():
        for copy in copies:
            copy.start()

    @pl.when(pl.program_id(0) == 0)
    def _():
        fill_bias(clips, valid_rows, valid_cols, bias)

    gather_rows(info, q_all, q_own[...], q_other[0])
    gather_rows(info, k_all, k_own[...], k_other[0])

    def find_logits(pair):
        first, count, offset = FIRST_KEY[pair], KEY_COUNT[pair], OFFSET[pair]
        query = q_all[pair * PAIR : (pair + 1) * PAIR, :]
        score = dot(k_all[first * TILE : (first + count) * TILE, :], query, NT)
        top = None
        for slot in range(count):
            rows = slice(slot * TILE, (slot + 1) * TILE)
            start = (offset + slot) * TILE
            part = score[rows, :] * (SCALE * LOG2E) + bias[start : start + TILE, :]
            logits_all[pair % 2, rows, :] = part
            part = jnp.max(part.reshape(TILE // 8, 8, PAIR), axis=0)
            top = part if top is None else jnp.maximum(top, part)
        return jnp.max(top, axis=0, keepdims=True)

    def find_probs(pair, top):
        count, offset = KEY_COUNT[pair], OFFSET[pair]
        logits = logits_all.at[pair % 2]
        total = None
        for slot in range(count):
            rows = slice(slot * TILE, (slot + 1) * TILE)
            weight = jnp.exp2(logits[rows, :] - top)
            logits[rows, :] = weight
            part = jnp.sum(weight.reshape(TILE // 8, 8, PAIR), axis=0)
            total = part if total is None else total + part
        inverse = 1.0 / jnp.sum(total, axis=0, keepdims=True)
        for slot in range(count):
            rows = slice(slot * TILE, (slot + 1) * TILE)
            start = (offset + slot) * TILE
            kept[start : start + TILE, :] = (logits[rows, :] * inverse).astype(jnp.bfloat16)

    top = find_logits(0)
    for pair in range(4):
        later = find_logits(pair + 1) if pair < 3 else None
        find_probs(pair, top)
        top = later

    @pl.when(step == pl.num_programs(0) - 1)
    def _():
        for copy in copies:
            copy.wait()


def probs_call(tables, q, k, others, begin, heads, passing, loads=()):
    def head_at(step, info):
        return lax.rem(info[MINE] + begin + step, 6)

    def other_block(which):
        return pl.BlockSpec(
            (1, LOCAL, HEAD_DIM), lambda step, info, *_: (which, 0, head_at(step, info))
        )

    own = pl.BlockSpec(
        (LOCAL, HEAD_DIM), lambda step, info, *_: (0, info[ME] * 6 + head_at(step, info))
    )
    block = (1, SLOTS * TILE, PAIR)
    anywhere = pl.BlockSpec(memory_space=pl.ANY)
    loaded = [jax.ShapeDtypeStruct((GROUP, DIM), jnp.bfloat16)] * (len(loads) // 2)
    return pl.pallas_call(
        functools.partial(probs_kernel, len(passing), len(loads)),
        out_shape=[jax.ShapeDtypeStruct((heads, SLOTS * TILE, PAIR), jnp.bfloat16)]
        + loaded
        + [jax.ShapeDtypeStruct(x.shape, x.dtype) for x in passing],
        grid_spec=pltpu.PrefetchScalarGridSpec(
            num_scalar_prefetch=4,
            grid=(heads,),
            in_specs=[own, own, other_block(0), other_block(1)]
            + [pl.BlockSpec(memory_space=pl.ANY)] * len(loads)
            + [anywhere] * len(passing),
            out_specs=[pl.BlockSpec(block, lambda step, *_: (step, 0, 0))]
            + [pl.BlockSpec(memory_space=pltpu.VMEM)] * len(loaded)
            + [anywhere] * len(passing),
            scratch_shapes=[
                pltpu.VMEM((GROUP, HEAD_DIM), jnp.bfloat16),
                pltpu.VMEM((GROUP, HEAD_DIM), jnp.bfloat16),
                pltpu.VMEM((SLOTS * TILE, PAIR), jnp.float32),
                pltpu.VMEM((2, KEY_MOST, PAIR), jnp.float32),
                pltpu.SemaphoreType.DMA((2,)),
            ],
        ),
        compiler_params=pltpu.CompilerParams(vmem_limit_bytes=VMEM),
        cost_estimate=pl.CostEstimate(
            flops=heads * 2 * SLOTS * TILE * PAIR * HEAD_DIM,
            bytes_accessed=2_000_000 * heads,
            transcendentals=heads * SLOTS * TILE * PAIR,
        ),
        input_output_aliases={
            8 + len(loads) + i: 1 + len(loaded) + i for i in range(len(passing))
        },
        name="probs",
    )(*tables, q, k, others, others, *loads, *passing)


def project(valid_rows, valid_cols, grad_all, grad_out, weight):
    cell = lax.broadcasted_iota(jnp.int32, (TILE, HEAD_DIM), 0)
    row, col = cell >> 4, cell & (TILE_W - 1)
    for half in range(2):
        grad = dot(grad_out[half * LOCAL : (half + 1) * LOCAL, :], weight, NT)
        for step in range(4):
            frame = half * 4 + step
            valid = (row < valid_rows[0, frame]) & (col < valid_cols[0, frame])
            rows = slice(frame * TILE, (frame + 1) * TILE)
            for head in range(2):
                part = grad[step * TILE : (step + 1) * TILE, head * TILE : (head + 1) * TILE]
                grad_all[head, rows, :] = jnp.where(valid, part, 0.0).astype(jnp.bfloat16)


def place_weight(info, pieces, refs, weight):
    for (slab, slots), ref in zip(pieces, refs):
        for index, slot in enumerate(slots):
            chunk = lax.rem(info[INNER] + SLOT_SHIFT[slot], 4)
            start = pl.multiple_of(slab * SLAB + chunk * CHUNK, 16)
            weight[pl.ds(start, CHUNK), :] = ref[index]


def head_copies(info, theirs, begin, heads, part, outs, sems, used):
    core, first = (1 - info[ME], info[THEIRS]) if theirs else (info[ME], info[MINE])
    copies = []
    for step in range(heads):
        head = core * 6 + lax.rem(first + begin + step, 6)
        cols = pl.ds(pl.multiple_of(head * HEAD_DIM, HEAD_DIM), HEAD_DIM)
        for index, out in enumerate(outs):
            copies.append(
                pltpu.make_async_copy(
                    part.at[index, :, step * HEAD_DIM : (step + 1) * HEAD_DIM],
                    out.at[:, cols],
                    sems.at[used + len(copies)],
                )
            )
    return copies


def grads_kernel(pieces, row_slot, placing, info, clips, valid_rows, valid_cols, *refs):
    weight_refs, refs = refs[: len(pieces)], refs[len(pieces) :]
    grad_out, probs = refs[:2]
    own_heads, other_heads = (refs[2:5], refs[5:8]), (refs[8:11], refs[11:14])
    earlier, refs = refs[14 : 14 + placing], refs[14 + placing :]
    (kept, sent), placed, refs = refs[:2], refs[2 : 2 + 3 * placing], refs[2 + 3 * placing :]
    weight, grad_all, q_all, k_all, v_all, grad_probs_all, grad_scores_all = refs[:7]
    dq_all, dk_all, dv_all = refs[7:10]
    me = info[ME]
    step = pl.program_id(0)
    copies = []
    for part in earlier:
        copies = head_copies(info, False, 0, 4, part, placed, refs[10], 0)

    @pl.when(step == 0)
    def _():
        for copy in copies:
            copy.start()
    probs_heads = [probs.at[2 * step + head] for head in range(2)]

    @pl.when(step == 0)
    def _():
        place_weight(info, pieces, weight_refs, weight)

    start = pl.multiple_of(info[row_slot] + step * PAIR, 64)
    rows = weight[pl.ds(start, PAIR), :]
    project(valid_rows, valid_cols, grad_all, grad_out, rows)
    for head in range(2):
        for scratch, own, other in zip(
            (q_all, k_all, v_all), own_heads[head], other_heads[head]
        ):
            gather_rows(info, scratch.at[head], own[...], other[0])

    def spans(pair):
        first, count = FIRST_KEY[pair], KEY_COUNT[pair]
        key_rows = slice(first * TILE, (first + count) * TILE)
        table_rows = slice(OFFSET[pair] * TILE, (OFFSET[pair] + count) * TILE)
        return key_rows, slice(pair * PAIR, (pair + 1) * PAIR), table_rows, count

    def find_grad_probs(item):
        head, pair = divmod(item, 4)
        key_rows, queries, _, count = spans(pair)
        grad_probs_all[item % 2, : count * TILE, :] = dot(
            v_all[head, key_rows, :], grad_all[head, queries, :], NT
        )

    def find_grad_scores(item):
        head, pair = divmod(item, 4)
        _, _, table_rows, count = spans(pair)
        grad_probs, grad_scores = grad_probs_all.at[item % 2], grad_scores_all.at[item % 2]
        probs = probs_heads[head]
        delta = None
        for slot in range(count):
            rows = slice(slot * TILE, (slot + 1) * TILE)
            start = table_rows.start + slot * TILE
            part = grad_probs[rows, :] * probs[start : start + TILE, :].astype(jnp.float32)
            part = jnp.sum(part.reshape(TILE // 8, 8, PAIR), axis=0)
            delta = part if delta is None else delta + part
        delta = jnp.sum(delta, axis=0, keepdims=True)
        for slot in range(count):
            rows = slice(slot * TILE, (slot + 1) * TILE)
            start = table_rows.start + slot * TILE
            weights = probs[start : start + TILE, :].astype(jnp.float32)
            grad_scores[rows, :] = (weights * (grad_probs[rows, :] - delta)).astype(jnp.bfloat16)

    def add_grads(item):
        head, pair = divmod(item, 4)
        key_rows, queries, table_rows, count = spans(pair)
        scores = grad_scores_all[item % 2, : count * TILE, :]
        dq_all[head, queries, :] = dot(scores, k_all[head, key_rows, :], TN)
        dk_all[head, key_rows, :] += dot(scores, q_all[head, queries, :], NN)
        dv_all[head, key_rows, :] += dot(
            probs_heads[head][table_rows, :], grad_all[head, queries, :], NN
        )

    def hand_over(head):
        cols = slice(head * HEAD_DIM, (head + 1) * HEAD_DIM)
        own = pl.ds(pl.multiple_of(me * LOCAL, LOCAL), LOCAL)
        other = pl.ds(pl.multiple_of((1 - me) * LOCAL, LOCAL), LOCAL)
        for index, (part, scale) in enumerate(((dq_all, SCALE), (dk_all, SCALE), (dv_all, 1.0))):
            kept[index, :, cols] = (part[head, own, :] * scale).astype(jnp.bfloat16)
            sent[index, :, cols] = (part[head, other, :] * scale).astype(jnp.bfloat16)

    dk_all[...] = jnp.zeros_like(dk_all)
    dv_all[...] = jnp.zeros_like(dv_all)
    find_grad_probs(0)
    for item in range(8):
        if item < 7:
            find_grad_probs(item + 1)
        if item > 0:
            add_grads(item - 1)
        find_grad_scores(item)
        if item == 5:
            hand_over(0)
    add_grads(7)
    hand_over(1)

    @pl.when(step == pl.num_programs(0) - 1)
    def _():
        for copy in copies:
            copy.wait()


def grads_call(tables, pieces, begin, heads, row_slot, tokens, probs, earlier=()):
    def head_at(parity, step, info):
        return lax.rem(info[MINE] + begin + 2 * step + parity, 6)

    def own_block(parity):
        return pl.BlockSpec(
            (LOCAL, HEAD_DIM),
            lambda step, info, *_: (0, info[ME] * 6 + head_at(parity, step, info)),
        )

    def other_block(parity, which):
        return pl.BlockSpec(
            (1, LOCAL, HEAD_DIM),
            lambda step, info, *_: (which, 0, head_at(parity, step, info)),
        )

    whole = pl.BlockSpec(memory_space=pltpu.VMEM)
    result = jax.ShapeDtypeStruct((3, LOCAL, heads * HEAD_DIM), jnp.bfloat16)
    full = jax.ShapeDtypeStruct((LOCAL, WIDTH), jnp.bfloat16)
    arrays = [piece for _, _, piece in pieces]
    layout = tuple((slab, slots) for slab, slots, _ in pieces)
    grad_out, *own, other = tokens
    return pl.pallas_call(
        functools.partial(grads_kernel, layout, row_slot, len(earlier)),
        out_shape=[result] * 2 + [full] * (3 * len(earlier)),
        grid_spec=pltpu.PrefetchScalarGridSpec(
            num_scalar_prefetch=4,
            grid=(heads // 2,),
            in_specs=[whole] * (len(arrays) + 2)
            + [own_block(parity) for parity in range(2) for _ in range(3)]
            + [other_block(parity, which) for parity in range(2) for which in range(3)]
            + [whole] * len(earlier),
            out_specs=[pl.BlockSpec((3, LOCAL, PAIR), lambda step, *_: (0, 0, step))] * 2
            + [pl.BlockSpec(memory_space=pl.ANY)] * (3 * len(earlier)),
            scratch_shapes=[
                pltpu.VMEM((3 * SLAB, DIM), jnp.bfloat16),
                pltpu.VMEM((2, GROUP, HEAD_DIM), jnp.bfloat16),
                pltpu.VMEM((2, GROUP, HEAD_DIM), jnp.bfloat16),
                pltpu.VMEM((2, GROUP, HEAD_DIM), jnp.bfloat16),
                pltpu.VMEM((2, GROUP, HEAD_DIM), jnp.bfloat16),
                pltpu.VMEM((2, KEY_MOST, PAIR), jnp.float32),
                pltpu.VMEM((2, KEY_MOST, PAIR), jnp.bfloat16),
                pltpu.VMEM((2, GROUP, HEAD_DIM), jnp.float32),
                pltpu.VMEM((2, GROUP, HEAD_DIM), jnp.float32),
                pltpu.VMEM((2, GROUP, HEAD_DIM), jnp.float32),
            ]
            + [pltpu.SemaphoreType.DMA((12,))] * len(earlier),
        ),
        compiler_params=pltpu.CompilerParams(vmem_limit_bytes=VMEM),
        cost_estimate=pl.CostEstimate(
            flops=heads * (8 * SLOTS * TILE * PAIR * HEAD_DIM + 2 * GROUP * HEAD_DIM * DIM),
            bytes_accessed=5_000_000 * heads,
            transcendentals=0,
        ),
        name="grads",
    )(*tables, *arrays, grad_out, probs, *own, *own, *[other] * 6, *earlier)


def merge_kernel(plan, count, info, *refs):
    parts, outs, sems = refs[count : count + len(plan)], refs[-4:-1], refs[-1]
    copies = []
    for part, (theirs, begin, heads) in zip(parts, plan):
        copies += head_copies(info, theirs, begin, heads, part, outs, sems, len(copies))
    for copy in copies:
        copy.start()
    for copy in copies:
        copy.wait()


def merge_call(info, earlier, parts):
    full = jax.ShapeDtypeStruct((LOCAL, WIDTH), jnp.bfloat16)
    plan = tuple(part[:3] for part in parts)
    copies = sum(3 * heads for _, _, heads in plan)
    return pl.pallas_call(
        functools.partial(merge_kernel, plan, len(earlier)),
        out_shape=[full] * 3,
        grid_spec=pltpu.PrefetchScalarGridSpec(
            num_scalar_prefetch=1,
            grid=(1,),
            in_specs=[pl.BlockSpec(memory_space=pl.ANY)] * len(earlier)
            + [pl.BlockSpec(memory_space=pltpu.VMEM)] * len(parts),
            out_specs=[pl.BlockSpec(memory_space=pl.ANY)] * 3,
            scratch_shapes=[pltpu.SemaphoreType.DMA((copies,))],
        ),
        input_output_aliases={1 + i: i for i in range(len(earlier))},
        compiler_params=pltpu.CompilerParams(vmem_limit_bytes=VMEM),
        name="merge",
    )(info, *earlier, *[part[3] for part in parts])


def place_table():
    table = np.zeros((NZ * NY * NX, 2, 6), np.int32)
    for dp in range(NZ * NY * NX):
        y, quarter = dp // NX % NY, dp // (NY * NX) % 4
        for core in range(2):
            outer, inner = (y, quarter) if core == 0 else (quarter, y)
            begin = (5, 0, 2, 3)
            rows = 64 * (1 - outer % 2)
            table[dp, core] = (core, begin[outer], begin[inner], inner, rows, 128 + rows)
    return table.reshape(-1, 6)


def place(z, y, x, core):
    return (((z % NZ) * NY + y % NY) * NX + x % NX) * 2 + core


def move(value, source):
    places = [
        (z, y, x, core) for z in range(NZ) for y in range(NY) for x in range(NX) for core in range(2)
    ]
    pairs = [(source(*taker), place(*taker)) for taker in places]
    return lax.ppermute(value, ("dp", "frame"), pairs)


def first_rows(step):
    def source(z, y, x, core):
        inner, outer = (z % 4, y) if core == 0 else (y, z % 4)
        return 128 * core + 8 * (4 * outer + inner) + 2 * x + ((z // 4) ^ step)

    return source


def along(last, distance):
    def source(z, y, x, core):
        if (core == 0) == last:
            return place(z, y + distance, x, core)
        return place(z + distance, y, x, core)

    return source


def line_rows(out_weight, z):
    x_lines = [
        [(z * NY + y) * NX + x for x in range(NX)] for z in range(NZ) for y in range(NY)
    ]
    even, odd = (move(out_weight, first_rows(step)) for step in range(2))
    rows = jnp.stack([jnp.where(z >= 4, odd, even), jnp.where(z >= 4, even, odd)])
    return lax.all_to_all(
        jnp.broadcast_to(rows[None], (NX,) + rows.shape),
        "dp",
        0,
        0,
        axis_index_groups=x_lines,
        tiled=True,
    ).reshape(1, CHUNK, DIM)


def beside_rows(rows):
    return [move(rows, along(False, distance)) for distance in (1, -1, 2)]


def far_slab(after_low, before_high):
    return move(after_low, along(True, 1)), move(before_high, along(True, -1))


def swap(value):
    return lax.ppermute(value, "frame", [(0, 1), (1, 0)])


def halves_kernel(info, *refs):
    values, out, sems = refs[:3], refs[3], refs[4]
    cols = pl.ds(pl.multiple_of((1 - info[ME]) * HALF, HALF), HALF)
    copies = [
        pltpu.make_async_copy(value.at[:, cols], out.at[index], sems.at[index])
        for index, value in enumerate(values)
    ]
    for copy in copies:
        copy.start()
    for copy in copies:
        copy.wait()


def other_halves(info, values):
    return pl.pallas_call(
        halves_kernel,
        out_shape=jax.ShapeDtypeStruct((3, LOCAL, HALF), jnp.bfloat16),
        grid_spec=pltpu.PrefetchScalarGridSpec(
            num_scalar_prefetch=1,
            grid=(1,),
            in_specs=[pl.BlockSpec(memory_space=pl.ANY)] * 3,
            out_specs=pl.BlockSpec(memory_space=pltpu.VMEM),
            scratch_shapes=[pltpu.SemaphoreType.DMA((3,))],
        ),
        compiler_params=pltpu.CompilerParams(vmem_limit_bytes=60 * 1024 * 1024),
        name="halves",
    )(info, *values)


def on_device(queries, keys, values, grad_out, out_weight, frame_clip, frame_rows, frame_cols):
    me = lax.axis_index("frame")
    dp = lax.axis_index("dp")
    info = lax.dynamic_index_in_dim(jnp.asarray(place_table()), dp * 2 + me, 0, keepdims=False)
    tables = (info, frame_clip, frame_rows, frame_cols)
    g_other = swap(grad_out)
    others = swap(other_halves(info, (queries, keys, values)))
    rows = line_rows(out_weight, dp // (NY * NX))
    slab = jnp.concatenate([rows] + beside_rows(rows))
    after_low, before_high = move(slab[:2], along(True, 1)), move(slab[2:], along(True, -1))
    attend = functools.partial(probs_call, tables, queries, keys, others)
    probs_early, g_all, slab = attend(0, 4, (slab,), (grad_out, g_other))
    after_high, before_low = move(slab[2:], along(True, 1)), move(slab[:2], along(True, -1))
    probs_late, after_low, before_high = attend(4, 2, (after_low, before_high))
    far_low, far_high = far_slab(after_low, before_high)
    tokens = (g_all, queries, keys, values, others)
    low, high, both = (0, 1), (2, 3), (0, 1, 2, 3)
    pieces = (
        (0, low, before_low),
        (0, high, before_high),
        (1, both, slab),
        (2, low, after_low),
        (2, high, after_high),
    )
    kept, sent = grads_call(tables, pieces, 0, 4, ROWS_EARLY, tokens, probs_early)
    arrived = swap(sent)
    pieces = (
        (0, low, after_low),
        (0, high, after_high),
        (1, low, far_low),
        (1, high, far_high),
        (2, low, before_low),
        (2, high, before_high),
    )
    kept_late, sent_late, *outs = grads_call(
        tables, pieces, 4, 2, ROWS_LATE, tokens, probs_late, (kept,)
    )
    arrived_late = swap(sent_late)
    parts = ((False, 4, 2, kept_late), (True, 0, 4, arrived))
    outs = merge_call(info, tuple(outs), parts)
    return tuple(merge_call(info, tuple(outs), ((True, 4, 2, arrived_late),)))


def solution(mesh):
    split = P(("dp", "frame"), None)
    table = P("dp", None)
    return jax.shard_map(
        on_device,
        mesh=mesh,
        in_specs=(split,) * 5 + (table,) * 3,
        out_specs=(split,) * 3,
        check_vma=False,
    )
```

```python
import functools

import jax
import jax.numpy as jnp
import numpy as np
from jax import lax
from jax.experimental import pallas as pl
from jax.experimental.pallas import tpu as pltpu
from jax.sharding import PartitionSpec as P

HEAD_DIM = 128
TILE_W = 16
TILE = 128
RADIUS = 3
FRAMES = 8
LOCAL = 512
GROUP = 1024
HALF = 768
WIDTH = 1536
DIM = 3072
PAIR = 2 * TILE
SCALE = 1.0 / HEAD_DIM**0.5
LOG2E = 1.4426950408889634

FIRST_KEY = (0, 0, 1, 3)
KEY_COUNT = (5, 7, 7, 5)
OFFSET = (0, 5, 12, 19)
SLOTS = 24
KEY_MOST = 7 * TILE
VMEM = 26 * 1024 * 1024

CHUNK = 48
SLAB = 192
NZ, NY, NX = 8, 4, 4
SLOT_SHIFT = (0, 1, 3, 2)
ME, MINE, THEIRS, INNER, ROWS_EARLY, ROWS_LATE = range(6)

NT = (((1,), (1,)), ((), ()))
TN = (((0,), (0,)), ((), ()))
NN = (((1,), (0,)), ((), ()))


def dot(lhs, rhs, dims):
    return lax.dot_general(lhs, rhs, dims, preferred_element_type=jnp.float32)


def fill_bias(clips, valid_rows, valid_cols, bias):
    key_cell = lax.broadcasted_iota(jnp.int32, (TILE, PAIR), 0)
    lane = lax.broadcasted_iota(jnp.int32, (TILE, PAIR), 1)
    query_cell = lane & (TILE - 1)
    key_row, key_col = key_cell >> 4, key_cell & (TILE_W - 1)
    near = (jnp.abs(key_row - (query_cell >> 4)) <= RADIUS) & (
        jnp.abs(key_col - (query_cell & (TILE_W - 1))) <= RADIUS
    )
    second = lane >= TILE
    for pair in range(4):
        left, right = 2 * pair, 2 * pair + 1
        for slot in range(KEY_COUNT[pair]):
            frame = FIRST_KEY[pair] + slot
            clip = clips[0, frame]
            left_same = (clips[0, left] == clip) & (abs(frame - left) <= RADIUS)
            right_same = (clips[0, right] == clip) & (abs(frame - right) <= RADIUS)
            linked = jnp.where(
                second, right_same.astype(jnp.int32), left_same.astype(jnp.int32)
            )
            allowed = (
                near
                & (linked > 0)
                & (key_row < valid_rows[0, frame])
                & (key_col < valid_cols[0, frame])
            )
            if frame == left:
                allowed = allowed | (key_cell == lane)
            if frame == right:
                allowed = allowed | (key_cell + TILE == lane)
            start = (OFFSET[pair] + slot) * TILE
            bias[start : start + TILE, :] = jnp.where(allowed, 0.0, -1e30)


def gather_rows(info, scratch, own, other):
    own_start = pl.multiple_of(info[ME] * LOCAL, LOCAL)
    other_start = pl.multiple_of((1 - info[ME]) * LOCAL, LOCAL)
    scratch[pl.ds(own_start, LOCAL), :] = own
    scratch[pl.ds(other_start, LOCAL), :] = other


def probs_kernel(
    passing, loading, info, clips, valid_rows, valid_cols, q_own, k_own, q_other, k_other, *refs
):
    loads, refs = refs[:loading], refs[loading + passing :]
    kept = refs[0].at[0]
    loaded, refs = refs[1 : 1 + loading // 2], refs[1 + loading // 2 + passing :]
    q_all, k_all, bias, logits_all = refs[:4]
    step = pl.program_id(0)
    copies = []
    for index, part in enumerate(loads):
        core = (info[ME], 1 - info[ME])[index]
        rows = pl.ds(pl.multiple_of(core * LOCAL, LOCAL), LOCAL)
        copies.append(pltpu.make_async_copy(part, loaded[0].at[rows, :], refs[4].at[index]))

    @pl.when(step == 0)
    def _():
        for copy in copies:
            copy.start()

    @pl.when(pl.program_id(0) == 0)
    def _():
        fill_bias(clips, valid_rows, valid_cols, bias)

    gather_rows(info, q_all, q_own[...], q_other[0])
    gather_rows(info, k_all, k_own[...], k_other[0])

    def find_logits(pair):
        first, count, offset = FIRST_KEY[pair], KEY_COUNT[pair], OFFSET[pair]
        query = q_all[pair * PAIR : (pair + 1) * PAIR, :]
        score = dot(k_all[first * TILE : (first + count) * TILE, :], query, NT)
        top = None
        for slot in range(count):
            rows = slice(slot * TILE, (slot + 1) * TILE)
            start = (offset + slot) * TILE
            part = score[rows, :] * (SCALE * LOG2E) + bias[start : start + TILE, :]
            logits_all[pair % 2, rows, :] = part
            part = jnp.max(part.reshape(TILE // 8, 8, PAIR), axis=0)
            top = part if top is None else jnp.maximum(top, part)
        return jnp.max(top, axis=0, keepdims=True)

    def find_probs(pair, top):
        count, offset = KEY_COUNT[pair], OFFSET[pair]
        logits = logits_all.at[pair % 2]
        total = None
        for slot in range(count):
            rows = slice(slot * TILE, (slot + 1) * TILE)
            weight = jnp.exp2(logits[rows, :] - top)
            logits[rows, :] = weight
            part = jnp.sum(weight.reshape(TILE // 8, 8, PAIR), axis=0)
            total = part if total is None else total + part
        inverse = 1.0 / jnp.sum(total, axis=0, keepdims=True)
        for slot in range(count):
            rows = slice(slot * TILE, (slot + 1) * TILE)
            start = (offset + slot) * TILE
            kept[start : start + TILE, :] = (logits[rows, :] * inverse).astype(jnp.bfloat16)

    top = find_logits(0)
    for pair in range(4):
        later = find_logits(pair + 1) if pair < 3 else None
        find_probs(pair, top)
        top = later

    @pl.when(step == pl.num_programs(0) - 1)
    def _():
        for copy in copies:
            copy.wait()


def probs_call(tables, q, k, others, begin, heads, passing, loads=()):
    def head_at(step, info):
        return lax.rem(info[MINE] + begin + step, 6)

    def other_block(which):
        return pl.BlockSpec(
            (1, LOCAL, HEAD_DIM), lambda step, info, *_: (which, 0, head_at(step, info))
        )

    own = pl.BlockSpec(
        (LOCAL, HEAD_DIM), lambda step, info, *_: (0, info[ME] * 6 + head_at(step, info))
    )
    block = (1, SLOTS * TILE, PAIR)
    anywhere = pl.BlockSpec(memory_space=pl.ANY)
    loaded = [jax.ShapeDtypeStruct((GROUP, DIM), jnp.bfloat16)] * (len(loads) // 2)
    return pl.pallas_call(
        functools.partial(probs_kernel, len(passing), len(loads)),
        out_shape=[jax.ShapeDtypeStruct((heads, SLOTS * TILE, PAIR), jnp.bfloat16)]
        + loaded
        + [jax.ShapeDtypeStruct(x.shape, x.dtype) for x in passing],
        grid_spec=pltpu.PrefetchScalarGridSpec(
            num_scalar_prefetch=4,
            grid=(heads,),
            in_specs=[own, own, other_block(0), other_block(1)]
            + [pl.BlockSpec(memory_space=pl.ANY)] * len(loads)
            + [anywhere] * len(passing),
            out_specs=[pl.BlockSpec(block, lambda step, *_: (step, 0, 0))]
            + [pl.BlockSpec(memory_space=pltpu.VMEM)] * len(loaded)
            + [anywhere] * len(passing),
            scratch_shapes=[
                pltpu.VMEM((GROUP, HEAD_DIM), jnp.bfloat16),
                pltpu.VMEM((GROUP, HEAD_DIM), jnp.bfloat16),
                pltpu.VMEM((SLOTS * TILE, PAIR), jnp.float32),
                pltpu.VMEM((2, KEY_MOST, PAIR), jnp.float32),
                pltpu.SemaphoreType.DMA((2,)),
            ],
        ),
        compiler_params=pltpu.CompilerParams(vmem_limit_bytes=VMEM),
        cost_estimate=pl.CostEstimate(
            flops=heads * 2 * SLOTS * TILE * PAIR * HEAD_DIM,
            bytes_accessed=2_000_000 * heads,
            transcendentals=heads * SLOTS * TILE * PAIR,
        ),
        input_output_aliases={
            8 + len(loads) + i: 1 + len(loaded) + i for i in range(len(passing))
        },
        name="probs",
    )(*tables, q, k, others, others, *loads, *passing)


def project(valid_rows, valid_cols, grad_all, grad_out, weight):
    cell = lax.broadcasted_iota(jnp.int32, (TILE, HEAD_DIM), 0)
    row, col = cell >> 4, cell & (TILE_W - 1)
    for half in range(2):
        grad = dot(grad_out[half * LOCAL : (half + 1) * LOCAL, :], weight, NT)
        for step in range(4):
            frame = half * 4 + step
            valid = (row < valid_rows[0, frame]) & (col < valid_cols[0, frame])
            rows = slice(frame * TILE, (frame + 1) * TILE)
            for head in range(2):
                part = grad[step * TILE : (step + 1) * TILE, head * TILE : (head + 1) * TILE]
                grad_all[head, rows, :] = jnp.where(valid, part, 0.0).astype(jnp.bfloat16)


def place_weight(info, pieces, refs, weight):
    for (slab, slots), ref in zip(pieces, refs):
        for index, slot in enumerate(slots):
            chunk = lax.rem(info[INNER] + SLOT_SHIFT[slot], 4)
            start = pl.multiple_of(slab * SLAB + chunk * CHUNK, 16)
            weight[pl.ds(start, CHUNK), :] = ref[index]


def head_copies(info, theirs, begin, heads, part, outs, sems, used):
    core, first = (1 - info[ME], info[THEIRS]) if theirs else (info[ME], info[MINE])
    copies = []
    for step in range(heads):
        head = core * 6 + lax.rem(first + begin + step, 6)
        cols = pl.ds(pl.multiple_of(head * HEAD_DIM, HEAD_DIM), HEAD_DIM)
        for index, out in enumerate(outs):
            copies.append(
                pltpu.make_async_copy(
                    part.at[index, :, step * HEAD_DIM : (step + 1) * HEAD_DIM],
                    out.at[:, cols],
                    sems.at[used + len(copies)],
                )
            )
    return copies


def grads_kernel(pieces, row_slot, placing, info, clips, valid_rows, valid_cols, *refs):
    weight_refs, refs = refs[: len(pieces)], refs[len(pieces) :]
    grad_out, probs = refs[:2]
    own_heads, other_heads = (refs[2:5], refs[5:8]), (refs[8:11], refs[11:14])
    earlier, refs = refs[14 : 14 + placing], refs[14 + placing :]
    (kept, sent), placed, refs = refs[:2], refs[2 : 2 + 3 * placing], refs[2 + 3 * placing :]
    weight, grad_all, q_all, k_all, v_all, grad_probs_all, grad_scores_all = refs[:7]
    dq_all, dk_all, dv_all = refs[7:10]
    me = info[ME]
    step = pl.program_id(0)
    copies = []
    for part in earlier:
        copies = head_copies(info, False, 0, 4, part, placed, refs[10], 0)

    @pl.when(step == 0)
    def _():
        for copy in copies:
            copy.start()
    probs_heads = [probs.at[2 * step + head] for head in range(2)]

    @pl.when(step == 0)
    def _():
        place_weight(info, pieces, weight_refs, weight)

    start = pl.multiple_of(info[row_slot] + step * PAIR, 64)
    rows = weight[pl.ds(start, PAIR), :]
    project(valid_rows, valid_cols, grad_all, grad_out, rows)
    for head in range(2):
        for scratch, own, other in zip(
            (q_all, k_all, v_all), own_heads[head], other_heads[head]
        ):
            gather_rows(info, scratch.at[head], own[...], other[0])

    def spans(pair):
        first, count = FIRST_KEY[pair], KEY_COUNT[pair]
        key_rows = slice(first * TILE, (first + count) * TILE)
        table_rows = slice(OFFSET[pair] * TILE, (OFFSET[pair] + count) * TILE)
        return key_rows, slice(pair * PAIR, (pair + 1) * PAIR), table_rows, count

    def find_grad_probs(item):
        head, pair = divmod(item, 4)
        key_rows, queries, _, count = spans(pair)
        grad_probs_all[item % 2, : count * TILE, :] = dot(
            v_all[head, key_rows, :], grad_all[head, queries, :], NT
        )

    def find_grad_scores(item):
        head, pair = divmod(item, 4)
        _, _, table_rows, count = spans(pair)
        grad_probs, grad_scores = grad_probs_all.at[item % 2], grad_scores_all.at[item % 2]
        probs = probs_heads[head]
        delta = None
        for slot in range(count):
            rows = slice(slot * TILE, (slot + 1) * TILE)
            start = table_rows.start + slot * TILE
            part = grad_probs[rows, :] * probs[start : start + TILE, :].astype(jnp.float32)
            part = jnp.sum(part.reshape(TILE // 8, 8, PAIR), axis=0)
            delta = part if delta is None else delta + part
        delta = jnp.sum(delta, axis=0, keepdims=True)
        for slot in range(count):
            rows = slice(slot * TILE, (slot + 1) * TILE)
            start = table_rows.start + slot * TILE
            weights = probs[start : start + TILE, :].astype(jnp.float32)
            grad_scores[rows, :] = (weights * (grad_probs[rows, :] - delta)).astype(jnp.bfloat16)

    def add_grads(item):
        head, pair = divmod(item, 4)
        key_rows, queries, table_rows, count = spans(pair)
        scores = grad_scores_all[item % 2, : count * TILE, :]
        dq_all[head, queries, :] = dot(scores, k_all[head, key_rows, :], TN)
        dk_all[head, key_rows, :] += dot(scores, q_all[head, queries, :], NN)
        dv_all[head, key_rows, :] += dot(
            probs_heads[head][table_rows, :], grad_all[head, queries, :], NN
        )

    def hand_over(head):
        cols = slice(head * HEAD_DIM, (head + 1) * HEAD_DIM)
        own = pl.ds(pl.multiple_of(me * LOCAL, LOCAL), LOCAL)
        other = pl.ds(pl.multiple_of((1 - me) * LOCAL, LOCAL), LOCAL)
        for index, (part, scale) in enumerate(((dq_all, SCALE), (dk_all, SCALE), (dv_all, 1.0))):
            kept[index, :, cols] = (part[head, own, :] * scale).astype(jnp.bfloat16)
            sent[index, :, cols] = (part[head, other, :] * scale).astype(jnp.bfloat16)

    dk_all[...] = jnp.zeros_like(dk_all)
    dv_all[...] = jnp.zeros_like(dv_all)
    find_grad_probs(0)
    for item in range(8):
        if item < 7:
            find_grad_probs(item + 1)
        if item > 0:
            add_grads(item - 1)
        find_grad_scores(item)
        if item == 5:
            hand_over(0)
    add_grads(7)
    hand_over(1)

    @pl.when(step == pl.num_programs(0) - 1)
    def _():
        for copy in copies:
            copy.wait()


def grads_call(tables, pieces, begin, heads, row_slot, tokens, probs, earlier=()):
    def head_at(parity, step, info):
        return lax.rem(info[MINE] + begin + 2 * step + parity, 6)

    def own_block(parity):
        return pl.BlockSpec(
            (LOCAL, HEAD_DIM),
            lambda step, info, *_: (0, info[ME] * 6 + head_at(parity, step, info)),
        )

    def other_block(parity, which):
        return pl.BlockSpec(
            (1, LOCAL, HEAD_DIM),
            lambda step, info, *_: (which, 0, head_at(parity, step, info)),
        )

    whole = pl.BlockSpec(memory_space=pltpu.VMEM)
    result = jax.ShapeDtypeStruct((3, LOCAL, heads * HEAD_DIM), jnp.bfloat16)
    full = jax.ShapeDtypeStruct((LOCAL, WIDTH), jnp.bfloat16)
    arrays = [piece for _, _, piece in pieces]
    layout = tuple((slab, slots) for slab, slots, _ in pieces)
    grad_out, *own, other = tokens
    return pl.pallas_call(
        functools.partial(grads_kernel, layout, row_slot, len(earlier)),
        out_shape=[result] * 2 + [full] * (3 * len(earlier)),
        grid_spec=pltpu.PrefetchScalarGridSpec(
            num_scalar_prefetch=4,
            grid=(heads // 2,),
            in_specs=[whole] * (len(arrays) + 2)
            + [own_block(parity) for parity in range(2) for _ in range(3)]
            + [other_block(parity, which) for parity in range(2) for which in range(3)]
            + [whole] * len(earlier),
            out_specs=[pl.BlockSpec((3, LOCAL, PAIR), lambda step, *_: (0, 0, step))] * 2
            + [pl.BlockSpec(memory_space=pl.ANY)] * (3 * len(earlier)),
            scratch_shapes=[
                pltpu.VMEM((3 * SLAB, DIM), jnp.bfloat16),
                pltpu.VMEM((2, GROUP, HEAD_DIM), jnp.bfloat16),
                pltpu.VMEM((2, GROUP, HEAD_DIM), jnp.bfloat16),
                pltpu.VMEM((2, GROUP, HEAD_DIM), jnp.bfloat16),
                pltpu.VMEM((2, GROUP, HEAD_DIM), jnp.bfloat16),
                pltpu.VMEM((2, KEY_MOST, PAIR), jnp.float32),
                pltpu.VMEM((2, KEY_MOST, PAIR), jnp.bfloat16),
                pltpu.VMEM((2, GROUP, HEAD_DIM), jnp.float32),
                pltpu.VMEM((2, GROUP, HEAD_DIM), jnp.float32),
                pltpu.VMEM((2, GROUP, HEAD_DIM), jnp.float32),
            ]
            + [pltpu.SemaphoreType.DMA((12,))] * len(earlier),
        ),
        compiler_params=pltpu.CompilerParams(vmem_limit_bytes=VMEM),
        cost_estimate=pl.CostEstimate(
            flops=heads * (8 * SLOTS * TILE * PAIR * HEAD_DIM + 2 * GROUP * HEAD_DIM * DIM),
            bytes_accessed=5_000_000 * heads,
            transcendentals=0,
        ),
        name="grads",
    )(*tables, *arrays, grad_out, probs, *own, *own, *[other] * 6, *earlier)


def merge_kernel(plan, count, info, *refs):
    parts, outs, sems = refs[count : count + len(plan)], refs[-4:-1], refs[-1]
    copies = []
    for part, (theirs, begin, heads) in zip(parts, plan):
        copies += head_copies(info, theirs, begin, heads, part, outs, sems, len(copies))
    for copy in copies:
        copy.start()
    for copy in copies:
        copy.wait()


def merge_call(info, earlier, parts):
    full = jax.ShapeDtypeStruct((LOCAL, WIDTH), jnp.bfloat16)
    plan = tuple(part[:3] for part in parts)
    copies = sum(3 * heads for _, _, heads in plan)
    return pl.pallas_call(
        functools.partial(merge_kernel, plan, len(earlier)),
        out_shape=[full] * 3,
        grid_spec=pltpu.PrefetchScalarGridSpec(
            num_scalar_prefetch=1,
            grid=(1,),
            in_specs=[pl.BlockSpec(memory_space=pl.ANY)] * len(earlier)
            + [pl.BlockSpec(memory_space=pltpu.VMEM)] * len(parts),
            out_specs=[pl.BlockSpec(memory_space=pl.ANY)] * 3,
            scratch_shapes=[pltpu.SemaphoreType.DMA((copies,))],
        ),
        input_output_aliases={1 + i: i for i in range(len(earlier))},
        compiler_params=pltpu.CompilerParams(vmem_limit_bytes=VMEM),
        name="merge",
    )(info, *earlier, *[part[3] for part in parts])


def place_table():
    table = np.zeros((NZ * NY * NX, 2, 6), np.int32)
    for dp in range(NZ * NY * NX):
        y, quarter = dp // NX % NY, dp // (NY * NX) % 4
        for core in range(2):
            outer, inner = (y, quarter) if core == 0 else (quarter, y)
            begin = (5, 0, 2, 3)
            rows = 64 * (1 - outer % 2)
            table[dp, core] = (core, begin[outer], begin[inner], inner, rows, 128 + rows)
    return table.reshape(-1, 6)


def place(z, y, x, core):
    return (((z % NZ) * NY + y % NY) * NX + x % NX) * 2 + core


def move(value, source):
    places = [
        (z, y, x, core) for z in range(NZ) for y in range(NY) for x in range(NX) for core in range(2)
    ]
    pairs = [(source(*taker), place(*taker)) for taker in places]
    return lax.ppermute(value, ("dp", "frame"), pairs)


def first_rows(step):
    def source(z, y, x, core):
        inner, outer = (z % 4, y) if core == 0 else (y, z % 4)
        return 128 * core + 8 * (4 * outer + inner) + 2 * x + ((z // 4) ^ step)

    return source


def along(last, distance):
    def source(z, y, x, core):
        if (core == 0) == last:
            return place(z, y + distance, x, core)
        return place(z + distance, y, x, core)

    return source


def line_rows(out_weight, z):
    x_lines = [
        [(z * NY + y) * NX + x for x in range(NX)] for z in range(NZ) for y in range(NY)
    ]
    even, odd = (move(out_weight, first_rows(step)) for step in range(2))
    rows = jnp.stack([jnp.where(z >= 4, odd, even), jnp.where(z >= 4, even, odd)])
    return lax.all_to_all(
        jnp.broadcast_to(rows[None], (NX,) + rows.shape),
        "dp",
        0,
        0,
        axis_index_groups=x_lines,
        tiled=True,
    ).reshape(1, CHUNK, DIM)


def beside_rows(rows):
    return [move(rows, along(False, distance)) for distance in (1, -1, 2)]


def far_slab(after_low, before_high):
    return move(after_low, along(True, 1)), move(before_high, along(True, -1))


def swap(value):
    return lax.ppermute(value, "frame", [(0, 1), (1, 0)])


def halves_kernel(*refs):
    values, out, sems = refs[:3], refs[3], refs[4]
    cols = pl.ds(pl.multiple_of((1 - lax.axis_index("frame")) * HALF, HALF), HALF)
    copies = [
        pltpu.make_async_copy(value.at[:, cols], out.at[index], sems.at[index])
        for index, value in enumerate(values)
    ]
    for copy in copies:
        copy.start()
    for copy in copies:
        copy.wait()


def other_halves(values):
    return pl.pallas_call(
        halves_kernel,
        out_shape=jax.ShapeDtypeStruct((3, LOCAL, HALF), jnp.bfloat16),
        in_specs=[pl.BlockSpec(memory_space=pl.ANY)] * 3,
        out_specs=pl.BlockSpec(memory_space=pltpu.VMEM),
        scratch_shapes=[pltpu.SemaphoreType.DMA((3,))],
        compiler_params=pltpu.CompilerParams(vmem_limit_bytes=60 * 1024 * 1024),
        name="halves",
    )(*values)


def on_device(queries, keys, values, grad_out, out_weight, frame_clip, frame_rows, frame_cols):
    me = lax.axis_index("frame")
    dp = lax.axis_index("dp")
    info = lax.dynamic_index_in_dim(jnp.asarray(place_table()), dp * 2 + me, 0, keepdims=False)
    tables = (info, frame_clip, frame_rows, frame_cols)
    g_other = swap(grad_out)
    others = swap(other_halves((queries, keys, values)))
    rows = line_rows(out_weight, dp // (NY * NX))
    slab = jnp.concatenate([rows] + beside_rows(rows))
    after_low, before_high = move(slab[:2], along(True, 1)), move(slab[2:], along(True, -1))
    attend = functools.partial(probs_call, tables, queries, keys, others)
    probs_early, g_all, slab = attend(0, 4, (slab,), (grad_out, g_other))
    after_high, before_low = move(slab[2:], along(True, 1)), move(slab[:2], along(True, -1))
    probs_late, after_low, before_high = attend(4, 2, (after_low, before_high))
    far_low, far_high = far_slab(after_low, before_high)
    tokens = (g_all, queries, keys, values, others)
    low, high, both = (0, 1), (2, 3), (0, 1, 2, 3)
    pieces = (
        (0, low, before_low),
        (0, high, before_high),
        (1, both, slab),
        (2, low, after_low),
        (2, high, after_high),
    )
    kept, sent = grads_call(tables, pieces, 0, 4, ROWS_EARLY, tokens, probs_early)
    arrived = swap(sent)
    pieces = (
        (0, low, after_low),
        (0, high, after_high),
        (1, low, far_low),
        (1, high, far_high),
        (2, low, before_low),
        (2, high, before_high),
    )
    kept_late, sent_late, *outs = grads_call(
        tables, pieces, 4, 2, ROWS_LATE, tokens, probs_late, (kept,)
    )
    arrived_late = swap(sent_late)
    parts = ((False, 4, 2, kept_late), (True, 0, 4, arrived))
    outs = merge_call(info, tuple(outs), parts)
    return tuple(merge_call(info, tuple(outs), ((True, 4, 2, arrived_late),)))


def solution(mesh):
    split = P(("dp", "frame"), None)
    table = P("dp", None)
    return jax.shard_map(
        on_device,
        mesh=mesh,
        in_specs=(split,) * 5 + (table,) * 3,
        out_specs=(split,) * 3,
        check_vma=False,
    )
```
